32 devices in a mesh: col: 8 (over z, y), row: 4 (over x, core).
Axes of the slice: x: 2, y: 2, z: 4, core: 2. Of those that a mesh axis runs over, the one named last changes fastest.
Arguments:
- latent: float32 [4096, 128], P('col'), may hold values from -6 to 6
- v_basis: float32 [8, 4, 16, 48, 256], P(None, 'row', 'col'), may hold values from -0.375 to 0.375
- u_basis: float32 [8, 4, 256, 768], P('col', 'row'), may hold values from -0.21875 to 0.21875
- ranks: int32 [8, 4, 16], P(None, 'row', 'col'), may hold values from 8 to 48, as said below
- slot_row: int32 [4, 8], P('row'), may hold values from 0 to 7, each once within a row
- wells: int32 [8, 4, 64], P('col', 'row'), may hold values from 0 to 255
- observed: float32 [8, 4, 64, 128], P('col', 'row'), may hold values from 0.3 to 2.5
Outputs:
- field: float32 [8, 4, 256, 128], P('col', 'row')
- gradient: float32 [4096, 128], P(('col', 'row'))
The draws below stay inside these ranges and needn't reach their ends.
Inputs may be any that keep to these rules, and one draw needn't show every extreme that they name: Each row of slot_row is a permutation of 0 .. 7. For every tile row, class and pair of tile columns 2i, 2i + 1, the two ranks sum to at most 72; in every class some pair reaches 72. `wells`: cells may repeat within a slot.
All inputs are finite; a program needn't handle non-finite values.
Results may differ from the reference program's by a relative error of at most 0.0003.
Values sent between devices are 32-bit elements; how exact they have to be, the bound alone decides.
No kernel may reach another device: no remote copies, remote signals or barrier semaphores. Data moves between devices by JAX's collectives and lax.ppermute only.
A program may use at most 128 MiB of HBM per device.

```python
import jax
import jax.numpy as jnp
from jax import lax

B = 256
K = 48
S = 128
WPT = 64
RPAIR = 72
TC = 16
RQ = 8
N_COL = 8
N_ROW = 4


def draw_ranks(key, part):
    lowest = K // 6
    key_first, key_second, key_flip = jax.random.split(jax.random.fold_in(key, 7), 3)
    shape = (RQ, N_ROW, TC // 2)
    first = jax.random.randint(key_first, shape, lowest, K + 1)
    upper = jnp.minimum(K, RPAIR - first)
    second = jax.random.randint(key_second, shape, lowest, upper + 1)
    row_index = jnp.arange(RQ, dtype=jnp.int32)[:, None, None]
    first = jnp.where(row_index == 0, K, jnp.where(row_index == 1, lowest, first))
    second = jnp.where(row_index == 0, RPAIR - K, second)
    flip = jax.random.randint(key_flip, shape, 0, 2)
    left = jnp.where(flip == 1, second, first)
    right = jnp.where(flip == 1, first, second)
    return jnp.stack([left, right], axis=-1).reshape(RQ, N_ROW, TC).astype(jnp.int32)


def set_ends(result, rng, low, high):
    shape = result.shape
    index_at = [jax.random.randint(jax.random.fold_in(rng, axis), (), 0, shape[axis]) for axis in range(len(shape))]
    result = result.at[tuple(index_at)].set(low)
    longest = shape.index(max(shape))
    index_at[longest] = (index_at[longest] + 1) % shape[longest]
    return result.at[tuple(index_at)].set(high)


def levels(key, extent, shards, smallest, largest):
    loudness = 1.0
    for dim, shards_of in shards:
        steps = jax.random.uniform(jax.random.fold_in(jax.random.fold_in(key, 6), dim), (shards_of,), jnp.float32, smallest / len(shards), largest / len(shards))
        loudness = loudness * jnp.repeat(jnp.exp(steps), extent[dim] // shards_of).reshape((-1,) + (1,) * (len(extent) - 1 - dim))
    return loudness


def centred(key, extent, width, most, shards=(), kind=jnp.bfloat16):
    drawn = width * jax.random.normal(key, extent, jnp.float32)
    if shards:
        drawn = drawn * levels(key, extent, shards, -0.22, 0.18)
    return jnp.clip(drawn, -most, most).astype(kind)


def setup_inputs(seed: int = 0) -> dict:
    streams_of = jax.random.split(jax.random.key(seed), 8)
    latent = centred(streams_of[0], (TC * B, S), 1.0, 6.0, ((0, 8),), jnp.float32)
    v_basis = centred(streams_of[1], (RQ, N_ROW, TC, K, B), B ** -0.5, 0.375, ((1, 4), (2, 8)), jnp.float32)
    u_basis = centred(streams_of[2], (N_COL, N_ROW, B, TC * K), (TC * K) ** -0.5, 0.21875, ((0, 8), (1, 4)), jnp.float32)
    ranks = draw_ranks(jax.random.fold_in(streams_of[7], 71), 0)
    slot_row = jax.vmap(lambda own: jax.random.permutation(own, N_COL))(jax.random.split(streams_of[4], N_ROW)).reshape((N_ROW, N_COL)).astype(jnp.int32)
    wells = set_ends(jax.random.randint(streams_of[5], (N_COL, N_ROW, WPT), 0, B), jax.random.fold_in(streams_of[5], 1), 0, B - 1).astype(jnp.int32)
    observed = jnp.clip(0.3 + 2.2 * jax.random.uniform(streams_of[6], (N_COL, N_ROW, WPT, S), jnp.float32) ** levels(streams_of[6], (N_COL, N_ROW, WPT, S), ((0, 8), (1, 4)), -0.2, 0.2), 0.3, 2.5)
    return {"latent": latent, "v_basis": v_basis, "u_basis": u_basis, "ranks": ranks, "slot_row": slot_row, "wells": wells, "observed": observed}


def reference(latent, v_basis, u_basis, ranks, slot_row, wells, observed):
    highest = lax.Precision.HIGHEST
    latent_tiles = latent.reshape(TC, B, S)
    u_flat = u_basis.reshape(N_COL * N_ROW, B, TC * K)
    wells_flat = wells.reshape(N_COL * N_ROW, WPT)
    observed_flat = observed.reshape(N_COL * N_ROW, WPT, S)
    rank_iota = jnp.arange(K, dtype=jnp.int32)
    cell_iota = jnp.arange(B, dtype=jnp.int32)

    def visit(accumulated, position):
        owner_col = position // N_ROW
        owner_class = position % N_ROW
        tile_row = slot_row[owner_class, owner_col]
        v_rows = v_basis[tile_row, owner_class]
        live_mask = (rank_iota[None, :] < ranks[tile_row, owner_class][:, None]).astype(jnp.float32)
        blocks = jnp.einsum('jkb,jbs->jks', v_rows, latent_tiles, precision=highest) * live_mask[:, :, None]
        u_owned = u_flat[position]
        field_block = jnp.dot(u_owned, blocks.reshape(TC * K, S), precision=highest)
        onehot = (wells_flat[position][:, None] == cell_iota[None, :]).astype(jnp.float32)
        at_wells = jnp.dot(onehot, field_block, precision=highest)
        expo_wells = jnp.exp(at_wells)
        weighted = (expo_wells - observed_flat[position]) * expo_wells / 0.25
        source = jnp.dot(onehot.T, weighted, precision=highest)
        adjoint = jnp.dot(u_owned.T, source, precision=highest).reshape(TC, K, S) * live_mask[:, :, None]
        accumulated = accumulated + jnp.einsum('jkb,jks->jbs', v_rows, adjoint, precision=highest)
        return accumulated, field_block

    accumulated, fields = lax.scan(visit, jnp.zeros((TC, B, S), jnp.float32),
                                   jnp.arange(N_COL * N_ROW, dtype=jnp.int32))
    gradient = latent + accumulated.reshape(TC * B, S)
    return fields.reshape(N_COL, N_ROW, B, S), gradient
```

```python
import functools

import jax
import jax.numpy as jnp
from jax import lax
from jax.experimental import pallas as pl
from jax.experimental.pallas import tpu as pltpu
from jax.sharding import PartitionSpec as P

F32 = jnp.float32
BF16 = jnp.bfloat16
VMEM = pl.BlockSpec(memory_space=pltpu.VMEM)
SMEM = pl.BlockSpec(memory_space=pltpu.SMEM)


def split(x):
    high = x.astype(BF16)
    low = (x - high.astype(F32)).astype(BF16)
    return high, low


def product(a, b, contract=(1, 0)):
    dims = (((contract[0],), (contract[1],)), ((), ()))
    a_high, a_low = split(a)
    b_high, b_low = split(b)
    both = lax.dot_general(a_high, jnp.concatenate([b_high, b_low], axis=1), dims, preferred_element_type=F32)
    width = b.shape[1]
    return both[:, :width] + both[:, width:] + lax.dot_general(a_low, b_high, dims, preferred_element_type=F32)


def repeat(count, body):
    if count == 1:
        body(0)
    else:
        pl.loop(0, count)(body)


def params(arrays):
    held = sum(a.size * a.dtype.itemsize for a in arrays)
    return pltpu.CompilerParams(vmem_limit_bytes=min(4 * held + (4 << 20), 56 << 20))


def blocks_kernel(group, order_ref, ranks_ref, latent_ref, v_ref, out_ref, held_ref):
    rows, local, rank_pad, cells = v_ref.shape
    width = latent_ref.shape[1]

    def some(g):
        for j in range(local):
            v_rows = v_ref[pl.ds(g * group, group), j].reshape(group * rank_pad, cells)
            made = product(v_rows, latent_ref[j * cells : (j + 1) * cells, :])
            held_ref[pl.ds(g * group, group), j] = made.reshape(group, rank_pad, width)

    repeat(rows // group, some)
    rank_index = lax.broadcasted_iota(jnp.int32, (rank_pad, width), 0)

    def place(g):
        for i in range(group):
            c = g * group + i
            q = order_ref[0, c]
            for j in range(local):
                live = rank_index < ranks_ref[q, j]
                out_ref[c, j * rank_pad : (j + 1) * rank_pad, :] = jnp.where(live, held_ref[q, j], 0.0)

    repeat(rows // group, place)


def owner_kernel(chunk, wells_ref, received_ref, u_ref, observed_ref, field_ref, adjoint_ref, at_wells_ref, rows_ref):
    depth = received_ref.shape[0]
    wells = observed_ref.shape[0]

    def first(k):
        part = product(u_ref[:, pl.ds(k * chunk, chunk)], received_ref[pl.ds(k * chunk, chunk), :])
        if depth == chunk:
            field_ref[...] = part
        else:

            @pl.when(k == 0)
            def _():
                field_ref[...] = part

            @pl.when(k > 0)
            def _():
                field_ref[...] += part

    repeat(depth // chunk, first)
    for w in range(wells):
        cell = wells_ref[0, 0, w]
        at_wells_ref[w : w + 1, :] = field_ref[pl.ds(cell, 1), :]
        rows_ref[w : w + 1, :] = u_ref[pl.ds(cell, 1), :]
    expo = jnp.exp(at_wells_ref[...])
    weighted = (expo - observed_ref[...]) * expo / 0.25

    def back(k):
        adjoint_ref[pl.ds(k * chunk, chunk), :] = product(rows_ref[:, pl.ds(k * chunk, chunk)], weighted, (0, 0))

    repeat(depth // chunk, back)


def gradient_kernel(
    group, axis, turn, order_ref, ranks_ref, returned_ref, v_ref, latent_ref, *refs
):
    out_refs, (ordered_ref, total_ref) = refs[:-2], refs[-2:]
    rows, local, rank_pad, cells = v_ref.shape
    width = latent_ref.shape[1]
    rank_index = lax.broadcasted_iota(jnp.int32, (rank_pad, width), 0)

    def place(g):
        for i in range(group):
            c = g * group + i
            q = order_ref[0, c]
            for j in range(local):
                live = rank_index < ranks_ref[q, j]
                ordered_ref[j, q] = jnp.where(live, returned_ref[c, j * rank_pad : (j + 1) * rank_pad, :], 0.0)

    repeat(rows // group, place)

    def some(g):
        for j in range(local):
            v_rows = v_ref[pl.ds(g * group, group), j].reshape(group * rank_pad, cells)
            part = product(v_rows, ordered_ref[j, pl.ds(g * group, group)].reshape(group * rank_pad, width), (0, 0))
            here = slice(j * cells, (j + 1) * cells)
            if rows == group:
                total_ref[here, :] = part
            else:

                @pl.when(g == 0)
                def _():
                    total_ref[here, :] = part

                @pl.when(g > 0)
                def _():
                    total_ref[here, :] += part

    repeat(rows // group, some)
    me = lax.axis_index(axis)
    size = out_refs[0].shape[0]
    for step, out_ref in enumerate(out_refs):
        there = pl.ds(pl.multiple_of(turn(me, step) * size, size), size)
        if step == 0:
            out_ref[...] = total_ref[there, :] + latent_ref[there, :]
        else:
            out_ref[...] = total_ref[there, :]


def on_device(n_row, latent, v_basis, u_basis, ranks, slot_row, wells, observed):
    rows, _, local, rank_pad, cells = v_basis.shape
    width = latent.shape[1]
    v_rows = v_basis[:, 0]
    ranks_here = ranks[:, 0]
    u_owned = u_basis[0, 0]
    observed_here = observed[0, 0]
    well_count = observed_here.shape[0]
    depth = u_owned.shape[1]
    group = 8 if rows % 8 == 0 else 1
    chunk = 768 if depth % 768 == 0 else depth
    sent = pl.pallas_call(
        functools.partial(blocks_kernel, group),
        out_shape=jax.ShapeDtypeStruct((rows, local * rank_pad, width), F32),
        in_specs=[SMEM, SMEM, VMEM, VMEM],
        out_specs=VMEM,
        scratch_shapes=[pltpu.VMEM((rows, local, rank_pad, width), F32)],
        compiler_params=params([latent, v_rows]),
        name="blocks",
    )(slot_row, ranks_here, latent, v_rows)
    received = lax.all_to_all(sent, "col", split_axis=0, concat_axis=0, tiled=True).reshape(depth, width)
    field, adjoint = pl.pallas_call(
        functools.partial(owner_kernel, chunk),
        out_shape=(jax.ShapeDtypeStruct((cells, width), F32), jax.ShapeDtypeStruct((depth, width), F32)),
        in_specs=[SMEM, VMEM, VMEM, VMEM],
        out_specs=(VMEM, VMEM),
        scratch_shapes=[pltpu.VMEM((well_count, width), F32), pltpu.VMEM((well_count, depth), F32)],
        compiler_params=params([received, u_owned, observed_here]),
        name="owner",
    )(wells, received, u_owned, observed_here)
    returned = lax.all_to_all(
        adjoint.reshape(rows, local * rank_pad, width), "col", split_axis=0, concat_axis=0, tiled=True
    )
    paired = n_row & (n_row - 1) == 0

    def turn(index, step):
        return index ^ step if paired else lax.rem(index + step, n_row)

    size = local * cells // n_row
    parts = pl.pallas_call(
        functools.partial(gradient_kernel, group, "row", turn),
        out_shape=[jax.ShapeDtypeStruct((size, width), F32)] * n_row,
        in_specs=[SMEM, SMEM, VMEM, VMEM, VMEM],
        out_specs=[VMEM] * n_row,
        scratch_shapes=[pltpu.VMEM((local, rows, rank_pad, width), F32), pltpu.VMEM((local * cells, width), F32)],
        compiler_params=params([returned, v_rows, latent]),
        name="gradient",
    )(slot_row, ranks_here, returned, v_rows, latent)
    gradient = parts[0]
    for step in range(1, n_row):
        pairs = [(i, i ^ step if paired else (i + step) % n_row) for i in range(n_row)]
        gradient = gradient + lax.ppermute(parts[step], "row", pairs)
    return field[None, None], gradient


def solution(mesh):
    placed = (
        P("col", None),
        P(None, "row", "col", None, None),
        P("col", "row", None, None),
        P(None, "row", "col"),
        P("row", None),
        P("col", "row", None),
        P("col", "row", None, None),
    )
    return jax.shard_map(
        functools.partial(on_device, mesh.shape["row"]),
        mesh=mesh,
        in_specs=placed,
        out_specs=(P("col", "row", None, None), P(("col", "row"), None)),
        check_vma=False,
    )
```

```python
import functools

import jax
import jax.numpy as jnp
from jax import lax
from jax.experimental import pallas as pl
from jax.experimental.pallas import tpu as pltpu
from jax.sharding import PartitionSpec as P

F32 = jnp.float32
BF16 = jnp.bfloat16
VMEM = pl.BlockSpec(memory_space=pltpu.VMEM)
SMEM = pl.BlockSpec(memory_space=pltpu.SMEM)
HBM = pl.BlockSpec(memory_space=pltpu.HBM)


def split(x):
    high = x.astype(BF16)
    low = (x - high.astype(F32)).astype(BF16)
    return high, low


def product(a, b, contract=(1, 0)):
    dims = (((contract[0],), (contract[1],)), ((), ()))
    a_high, a_low = split(a)
    b_high, b_low = split(b)
    both = lax.dot_general(a_high, jnp.concatenate([b_high, b_low], axis=1), dims, preferred_element_type=F32)
    width = b.shape[1]
    return both[:, :width] + both[:, width:] + lax.dot_general(a_low, b_high, dims, preferred_element_type=F32)


def repeat(count, body):
    if count == 1:
        body(0)
    else:
        pl.loop(0, count)(body)


def params(arrays):
    held = sum(a.size * a.dtype.itemsize for a in arrays)
    return pltpu.CompilerParams(vmem_limit_bytes=min(4 * held + (4 << 20), 56 << 20))


def stay(x):
    return pltpu.with_memory_space_constraint(x, pltpu.HBM)


def blocks_kernel(
    group, order_hbm, ranks_hbm, latent_hbm, v_hbm, out_ref, held_ref, order_ref, ranks_ref, latent_ref, v_ref, sems
):
    local, rows, rank_pad, cells = v_ref.shape
    width = latent_ref.shape[1]
    small = [
        pltpu.make_async_copy(order_hbm, order_ref, sems.at[2 * local]),
        pltpu.make_async_copy(ranks_hbm, ranks_ref, sems.at[2 * local + 1]),
    ]
    tiles = []
    for j in range(local):
        here = pl.ds(j * cells, cells)
        tiles.append(
            (
                pltpu.make_async_copy(v_hbm.at[:, j], v_ref.at[j], sems.at[2 * j]),
                pltpu.make_async_copy(latent_hbm.at[here], latent_ref.at[here], sems.at[2 * j + 1]),
            )
        )
    for copies in tiles:
        for copy in copies:
            copy.start()
    for copy in small:
        copy.start()
    for j in range(local):
        for copy in tiles[j]:
            copy.wait()

        def some(g):
            v_rows = v_ref[j, pl.ds(g * group, group)].reshape(group * rank_pad, cells)
            made = product(v_rows, latent_ref[j * cells : (j + 1) * cells, :])
            held_ref[j, pl.ds(g * group, group)] = made.reshape(group, rank_pad, width)

        repeat(rows // group, some)
    for copy in small:
        copy.wait()
    rank_index = lax.broadcasted_iota(jnp.int32, (rank_pad, width), 0)

    def place(g):
        for i in range(group):
            c = g * group + i
            q = order_ref[0, c]
            for j in range(local):
                live = rank_index < ranks_ref[j, q]
                out_ref[c, j * rank_pad : (j + 1) * rank_pad, :] = jnp.where(live, held_ref[j, q], 0.0)

    repeat(rows // group, place)


def owner_kernel(
    chunk, wells_hbm, received_ref, u_ref, observed_ref, field_ref, adjoint_ref, at_wells_ref, rows_ref, wells_ref, sem
):
    depth = received_ref.shape[0]
    copy = pltpu.make_async_copy(wells_hbm, wells_ref, sem)
    copy.start()
    wells = observed_ref.shape[0]

    def first(k):
        part = product(u_ref[:, pl.ds(k * chunk, chunk)], received_ref[pl.ds(k * chunk, chunk), :])
        if depth == chunk:
            field_ref[...] = part
        else:

            @pl.when(k == 0)
            def _():
                field_ref[...] = part

            @pl.when(k > 0)
            def _():
                field_ref[...] += part

    repeat(depth // chunk, first)
    copy.wait()
    for w in range(wells):
        cell = wells_ref[0, w]
        at_wells_ref[w : w + 1, :] = field_ref[pl.ds(cell, 1), :]
        rows_ref[w : w + 1, :] = u_ref[pl.ds(cell, 1), :]
    expo = jnp.exp(at_wells_ref[...])
    weighted = (expo - observed_ref[...]) * expo / 0.25

    def back(k):
        adjoint_ref[pl.ds(k * chunk, chunk), :] = product(rows_ref[:, pl.ds(k * chunk, chunk)], weighted, (0, 0))

    repeat(depth // chunk, back)


def gradient_kernel(
    group, axis, turn, order_ref, ranks_ref, returned_ref, v_ref, latent_ref, *refs
):
    out_refs, (ordered_ref, total_ref) = refs[:-2], refs[-2:]
    rows, local, rank_pad, cells = v_ref.shape
    width = latent_ref.shape[1]
    rank_index = lax.broadcasted_iota(jnp.int32, (rank_pad, width), 0)

    def place(g):
        for i in range(group):
            c = g * group + i
            q = order_ref[0, c]
            for j in range(local):
                live = rank_index < ranks_ref[j, q]
                ordered_ref[j, q] = jnp.where(live, returned_ref[c, j * rank_pad : (j + 1) * rank_pad, :], 0.0)

    repeat(rows // group, place)

    def some(g):
        for j in range(local):
            v_rows = v_ref[pl.ds(g * group, group), j].reshape(group * rank_pad, cells)
            part = product(v_rows, ordered_ref[j, pl.ds(g * group, group)].reshape(group * rank_pad, width), (0, 0))
            here = slice(j * cells, (j + 1) * cells)
            if rows == group:
                total_ref[here, :] = part
            else:

                @pl.when(g == 0)
                def _():
                    total_ref[here, :] = part

                @pl.when(g > 0)
                def _():
                    total_ref[here, :] += part

    repeat(rows // group, some)
    me = lax.axis_index(axis)
    size = out_refs[0].shape[0]
    for step, out_ref in enumerate(out_refs):
        there = pl.ds(pl.multiple_of(turn(me, step) * size, size), size)
        if step == 0:
            out_ref[...] = total_ref[there, :] + latent_ref[there, :]
        else:
            out_ref[...] = total_ref[there, :]


def on_device(n_row, latent, v_basis, u_basis, ranks, slot_row, wells, observed):
    rows, _, local, rank_pad, cells = v_basis.shape
    width = latent.shape[1]
    v_rows = v_basis[:, 0]
    ranks_here = ranks[:, 0].T
    u_owned = u_basis[0, 0]
    observed_here = observed[0, 0]
    well_count = observed_here.shape[0]
    depth = u_owned.shape[1]
    group = 8 if rows % 8 == 0 else 1
    chunk = 768 if depth % 768 == 0 else depth
    sent = pl.pallas_call(
        functools.partial(blocks_kernel, group),
        out_shape=jax.ShapeDtypeStruct((rows, local * rank_pad, width), F32),
        in_specs=[HBM, HBM, HBM, HBM],
        out_specs=VMEM,
        scratch_shapes=[
            pltpu.VMEM((local, rows, rank_pad, width), F32),
            pltpu.SMEM(slot_row.shape, jnp.int32),
            pltpu.SMEM(ranks_here.shape, jnp.int32),
            pltpu.VMEM(latent.shape, F32),
            pltpu.VMEM((local, rows, rank_pad, cells), F32),
            pltpu.SemaphoreType.DMA((2 * local + 2,)),
        ],
        compiler_params=params([latent, v_rows]),
        name="blocks",
    )(stay(slot_row), stay(ranks_here), stay(latent), stay(v_rows))
    received = lax.all_to_all(sent, "col", split_axis=0, concat_axis=0, tiled=True).reshape(depth, width)
    field, adjoint = pl.pallas_call(
        functools.partial(owner_kernel, chunk),
        out_shape=(jax.ShapeDtypeStruct((cells, width), F32), jax.ShapeDtypeStruct((depth, width), F32)),
        in_specs=[HBM, VMEM, VMEM, VMEM],
        out_specs=(VMEM, VMEM),
        scratch_shapes=[
            pltpu.VMEM((well_count, width), F32),
            pltpu.VMEM((well_count, depth), F32),
            pltpu.SMEM((1, well_count), jnp.int32),
            pltpu.SemaphoreType.DMA,
        ],
        compiler_params=params([received, u_owned, observed_here]),
        name="owner",
    )(stay(wells[0]), received, u_owned, observed_here)
    returned = lax.all_to_all(
        adjoint.reshape(rows, local * rank_pad, width), "col", split_axis=0, concat_axis=0, tiled=True
    )
    paired = n_row & (n_row - 1) == 0

    def turn(index, step):
        return index ^ step if paired else lax.rem(index + step, n_row)

    size = local * cells // n_row
    parts = pl.pallas_call(
        functools.partial(gradient_kernel, group, "row", turn),
        out_shape=[jax.ShapeDtypeStruct((size, width), F32)] * n_row,
        in_specs=[SMEM, SMEM, VMEM, VMEM, VMEM],
        out_specs=[VMEM] * n_row,
        scratch_shapes=[pltpu.VMEM((local, rows, rank_pad, width), F32), pltpu.VMEM((local * cells, width), F32)],
        compiler_params=params([returned, v_rows, latent]),
        name="gradient",
    )(slot_row, ranks_here, returned, v_rows, latent)
    gradient = parts[0]
    for step in range(1, n_row):
        pairs = [(i, i ^ step if paired else (i + step) % n_row) for i in range(n_row)]
        gradient = gradient + lax.ppermute(parts[step], "row", pairs)
    return field[None, None], gradient


def solution(mesh):
    placed = (
        P("col", None),
        P(None, "row", "col", None, None),
        P("col", "row", None, None),
        P(None, "row", "col"),
        P("row", None),
        P("col", "row", None),
        P("col", "row", None, None),
    )
    return jax.shard_map(
        functools.partial(on_device, mesh.shape["row"]),
        mesh=mesh,
        in_specs=placed,
        out_specs=(P("col", "row", None, None), P(("col", "row"), None)),
        check_vma=False,
    )
```

```python
import functools

import jax
import jax.numpy as jnp
from jax import lax
from jax.experimental import pallas as pl
from jax.experimental.pallas import tpu as pltpu
from jax.sharding import PartitionSpec as P

F32 = jnp.float32
BF16 = jnp.bfloat16
VMEM = pl.BlockSpec(memory_space=pltpu.VMEM)
SMEM = pl.BlockSpec(memory_space=pltpu.SMEM)
HBM = pl.BlockSpec(memory_space=pltpu.HBM)
MARK = 8


def split(x):
    high = x.astype(BF16)
    low = (x - high.astype(F32)).astype(BF16)
    return high, low


def product(a, b, contract=(1, 0)):
    dims = (((contract[0],), (contract[1],)), ((), ()))
    a_high, a_low = split(a)
    b_high, b_low = split(b)
    both = lax.dot_general(a_high, jnp.concatenate([b_high, b_low], axis=1), dims, preferred_element_type=F32)
    width = b.shape[1]
    return both[:, :width] + both[:, width:] + lax.dot_general(a_low, b_high, dims, preferred_element_type=F32)


def repeat(count, body):
    if count == 1:
        body(0)
    else:
        pl.loop(0, count)(body)


def each(count, body):
    if count <= 16:
        for i in range(count):
            body(i)
    else:
        pl.loop(0, count)(body)


def params(arrays):
    held = sum(a.size * a.dtype.itemsize for a in arrays)
    return pltpu.CompilerParams(vmem_limit_bytes=min(4 * held + (4 << 20), 56 << 20))


def packed_rows(rank_pad):
    return rank_pad + rank_pad // 2


def lengthen(x, size):
    return jnp.concatenate([x, jnp.zeros((size - x.shape[0], x.shape[1]), x.dtype)], axis=0)


def stay(x):
    return pltpu.with_memory_space_constraint(x, pltpu.HBM)


def blocks_kernel(
    group, order_hbm, ranks_hbm, latent_hbm, v_hbm, out_ref, held_ref, order_ref, ranks_ref, latent_ref, v_ref, sems
):
    local, rows, rank_pad, cells = v_ref.shape
    width = latent_ref.shape[1]
    small = [
        pltpu.make_async_copy(order_hbm, order_ref, sems.at[2 * local]),
        pltpu.make_async_copy(ranks_hbm, ranks_ref, sems.at[2 * local + 1]),
    ]
    tiles = []
    for j in range(local):
        here = pl.ds(j * cells, cells)
        tiles.append(
            (
                pltpu.make_async_copy(v_hbm.at[:, j], v_ref.at[j], sems.at[2 * j]),
                pltpu.make_async_copy(latent_hbm.at[here], latent_ref.at[here], sems.at[2 * j + 1]),
            )
        )
    for copies in tiles:
        for copy in copies:
            copy.start()
    for copy in small:
        copy.start()
    for j in range(local):
        for copy in tiles[j]:
            copy.wait()

        def some(g):
            v_rows = v_ref[j, pl.ds(g * group, group)].reshape(group * rank_pad, cells)
            made = product(v_rows, latent_ref[j * cells : (j + 1) * cells, :])
            held_ref[j, pl.ds(g * group, group)] = made.reshape(group, rank_pad, width)

        repeat(rows // group, some)
    for copy in small:
        copy.wait()
    rank_index = lax.broadcasted_iota(jnp.int32, (rank_pad, width), 0)
    size = packed_rows(rank_pad)

    def place(g):
        for i in range(group):
            c = g * group + i
            q = order_ref[0, c]
            for pair in range(local // 2):
                left, right = 2 * pair, 2 * pair + 1
                cut = ranks_ref[left, q]
                first = jnp.where(rank_index < cut, held_ref[left, q], 0.0)
                second = jnp.where(rank_index < ranks_ref[right, q], held_ref[right, q], 0.0)
                base = pair * (size + MARK)
                out_ref[c, base : base + size, :] = lengthen(first, size) + pltpu.roll(lengthen(second, size), cut, 0)
                out_ref[c, base + size : base + size + MARK, :] = jnp.full((MARK, width), cut.astype(F32))

    repeat(rows // group, place)


def owner_kernel(
    chunk,
    rank_pad,
    wells_hbm,
    received_ref,
    u_ref,
    observed_ref,
    field_ref,
    packed_ref,
    stacked_ref,
    at_wells_ref,
    rows_ref,
    wells_ref,
    sem,
):
    sources = received_ref.shape[0]
    depth, width = stacked_ref.shape
    wells = observed_ref.shape[0]
    size = packed_rows(rank_pad)
    pairs = received_ref.shape[1] // (size + MARK)
    copy = pltpu.make_async_copy(wells_hbm, wells_ref, sem)
    copy.start()
    rank_index = lax.broadcasted_iota(jnp.int32, (rank_pad, width), 0)
    packed_index = lax.broadcasted_iota(jnp.int32, (size, width), 0)

    def first_rank(c, pair):
        at = pair * (size + MARK) + size
        return received_ref[c, at : at + 1, :][0, 0].astype(jnp.int32)

    def unpack(c):
        for pair in range(pairs):
            cut = first_rank(c, pair)
            both = received_ref[c, pair * (size + MARK) : pair * (size + MARK) + size, :]
            left = pl.multiple_of((c * pairs + pair) * 2 * rank_pad, 8)
            stacked_ref[pl.ds(left, rank_pad), :] = jnp.where(rank_index < cut, both[:rank_pad], 0.0)
            second = pltpu.roll(both, size - cut, 0)[:rank_pad]
            right = pl.multiple_of(left + rank_pad, 8)
            stacked_ref[pl.ds(right, rank_pad), :] = jnp.where(rank_index < size - cut, second, 0.0)

    def pack(c):
        for pair in range(pairs):
            cut = first_rank(c, pair)
            left = pl.multiple_of((c * pairs + pair) * 2 * rank_pad, 8)
            first = lengthen(stacked_ref[pl.ds(left, rank_pad), :], size)
            right = pl.multiple_of(left + rank_pad, 8)
            second = pltpu.roll(lengthen(stacked_ref[pl.ds(right, rank_pad), :], size), cut, 0)
            packed_ref[c, pair * size : (pair + 1) * size, :] = jnp.where(packed_index < cut, first, second)

    each(sources, unpack)

    def first(k):
        part = product(u_ref[:, pl.ds(k * chunk, chunk)], stacked_ref[pl.ds(k * chunk, chunk), :])
        if depth == chunk:
            field_ref[...] = part
        else:

            @pl.when(k == 0)
            def _():
                field_ref[...] = part

            @pl.when(k > 0)
            def _():
                field_ref[...] += part

    repeat(depth // chunk, first)
    copy.wait()
    for w in range(wells):
        cell = wells_ref[0, w]
        at_wells_ref[w : w + 1, :] = field_ref[pl.ds(cell, 1), :]
        rows_ref[w : w + 1, :] = u_ref[pl.ds(cell, 1), :]
    expo = jnp.exp(at_wells_ref[...])
    weighted = (expo - observed_ref[...]) * expo / 0.25

    def back(k):
        stacked_ref[pl.ds(k * chunk, chunk), :] = product(rows_ref[:, pl.ds(k * chunk, chunk)], weighted, (0, 0))

    repeat(depth // chunk, back)
    each(sources, pack)


def gradient_kernel(
    group, axis, turn, order_ref, ranks_ref, returned_ref, v_ref, latent_ref, *refs
):
    out_refs, (ordered_ref, total_ref) = refs[:-2], refs[-2:]
    rows, local, rank_pad, cells = v_ref.shape
    width = latent_ref.shape[1]
    rank_index = lax.broadcasted_iota(jnp.int32, (rank_pad, width), 0)

    packed = packed_rows(rank_pad)

    def place(g):
        for i in range(group):
            c = g * group + i
            q = order_ref[0, c]
            for pair in range(local // 2):
                left, right = 2 * pair, 2 * pair + 1
                cut = ranks_ref[left, q]
                both = returned_ref[c, pair * packed : (pair + 1) * packed, :]
                ordered_ref[left, q] = jnp.where(rank_index < cut, both[:rank_pad], 0.0)
                second = pltpu.roll(both, packed - cut, 0)[:rank_pad]
                ordered_ref[right, q] = jnp.where(rank_index < ranks_ref[right, q], second, 0.0)

    repeat(rows // group, place)

    def some(g):
        for j in range(local):
            v_rows = v_ref[pl.ds(g * group, group), j].reshape(group * rank_pad, cells)
            part = product(v_rows, ordered_ref[j, pl.ds(g * group, group)].reshape(group * rank_pad, width), (0, 0))
            here = slice(j * cells, (j + 1) * cells)
            if rows == group:
                total_ref[here, :] = part
            else:

                @pl.when(g == 0)
                def _():
                    total_ref[here, :] = part

                @pl.when(g > 0)
                def _():
                    total_ref[here, :] += part

    repeat(rows // group, some)
    me = lax.axis_index(axis)
    size = out_refs[0].shape[0]
    for step, out_ref in enumerate(out_refs):
        there = pl.ds(pl.multiple_of(turn(me, step) * size, size), size)
        if step == 0:
            out_ref[...] = total_ref[there, :] + latent_ref[there, :]
        else:
            out_ref[...] = total_ref[there, :]


def on_device(n_row, latent, v_basis, u_basis, ranks, slot_row, wells, observed):
    rows, _, local, rank_pad, cells = v_basis.shape
    width = latent.shape[1]
    v_rows = v_basis[:, 0]
    ranks_here = ranks[:, 0].T
    u_owned = u_basis[0, 0]
    observed_here = observed[0, 0]
    well_count = observed_here.shape[0]
    pairs, packed = local // 2, packed_rows(rank_pad)
    depth = u_owned.shape[1]
    group = 8 if rows % 8 == 0 else 1
    chunk = 768 if depth % 768 == 0 else depth
    sent = pl.pallas_call(
        functools.partial(blocks_kernel, group),
        out_shape=jax.ShapeDtypeStruct((rows, pairs * (packed + MARK), width), F32),
        in_specs=[HBM, HBM, HBM, HBM],
        out_specs=VMEM,
        scratch_shapes=[
            pltpu.VMEM((local, rows, rank_pad, width), F32),
            pltpu.SMEM(slot_row.shape, jnp.int32),
            pltpu.SMEM(ranks_here.shape, jnp.int32),
            pltpu.VMEM(latent.shape, F32),
            pltpu.VMEM((local, rows, rank_pad, cells), F32),
            pltpu.SemaphoreType.DMA((2 * local + 2,)),
        ],
        compiler_params=params([latent, v_rows]),
        name="blocks",
    )(stay(slot_row), stay(ranks_here), stay(latent), stay(v_rows))
    received = lax.all_to_all(sent, "col", split_axis=0, concat_axis=0, tiled=True)
    field, adjoint = pl.pallas_call(
        functools.partial(owner_kernel, chunk, rank_pad),
        out_shape=(
            jax.ShapeDtypeStruct((cells, width), F32),
            jax.ShapeDtypeStruct((rows, pairs * packed, width), F32),
        ),
        in_specs=[HBM, VMEM, VMEM, VMEM],
        out_specs=(VMEM, VMEM),
        scratch_shapes=[
            pltpu.VMEM((depth, width), F32),
            pltpu.VMEM((well_count, width), F32),
            pltpu.VMEM((well_count, depth), F32),
            pltpu.SMEM((1, well_count), jnp.int32),
            pltpu.SemaphoreType.DMA,
        ],
        compiler_params=params([received, u_owned, observed_here]),
        name="owner",
    )(stay(wells[0]), received, u_owned, observed_here)
    returned = lax.all_to_all(adjoint, "col", split_axis=0, concat_axis=0, tiled=True)
    paired = n_row & (n_row - 1) == 0

    def turn(index, step):
        return index ^ step if paired else lax.rem(index + step, n_row)

    size = local * cells // n_row
    parts = pl.pallas_call(
        functools.partial(gradient_kernel, group, "row", turn),
        out_shape=[jax.ShapeDtypeStruct((size, width), F32)] * n_row,
        in_specs=[SMEM, SMEM, VMEM, VMEM, VMEM],
        out_specs=[VMEM] * n_row,
        scratch_shapes=[pltpu.VMEM((local, rows, rank_pad, width), F32), pltpu.VMEM((local * cells, width), F32)],
        compiler_params=params([returned, v_rows, latent]),
        name="gradient",
    )(slot_row, ranks_here, returned, v_rows, latent)
    gradient = parts[0]
    for step in range(1, n_row):
        pairs = [(i, i ^ step if paired else (i + step) % n_row) for i in range(n_row)]
        gradient = gradient + lax.ppermute(parts[step], "row", pairs)
    return field[None, None], gradient


def solution(mesh):
    placed = (
        P("col", None),
        P(None, "row", "col", None, None),
        P("col", "row", None, None),
        P(None, "row", "col"),
        P("row", None),
        P("col", "row", None),
        P("col", "row", None, None),
    )
    return jax.shard_map(
        functools.partial(on_device, mesh.shape["row"]),
        mesh=mesh,
        in_specs=placed,
        out_specs=(P("col", "row", None, None), P(("col", "row"), None)),
        check_vma=False,
    )
```

```python
import functools

import jax
import jax.numpy as jnp
from jax import lax
from jax.experimental import pallas as pl
from jax.experimental.pallas import tpu as pltpu
from jax.sharding import PartitionSpec as P

F32 = jnp.float32
BF16 = jnp.bfloat16
VMEM = pl.BlockSpec(memory_space=pltpu.VMEM)
HBM = pl.BlockSpec(memory_space=pltpu.HBM)
MARK = 8


def split(x):
    high = x.astype(BF16)
    low = (x - high.astype(F32)).astype(BF16)
    return high, low


def product(a, b, contract=(1, 0)):
    dims = (((contract[0],), (contract[1],)), ((), ()))
    a_high, a_low = split(a)
    b_high, b_low = split(b)
    both = lax.dot_general(a_high, jnp.concatenate([b_high, b_low], axis=1), dims, preferred_element_type=F32)
    width = b.shape[1]
    return both[:, :width] + both[:, width:] + lax.dot_general(a_low, b_high, dims, preferred_element_type=F32)


def repeat(count, body):
    if count == 1:
        body(0)
    else:
        pl.loop(0, count)(body)


def each(count, body):
    if count <= 16:
        for i in range(count):
            body(i)
    else:
        pl.loop(0, count)(body)


def params(arrays):
    held = sum(a.size * a.dtype.itemsize for a in arrays)
    return pltpu.CompilerParams(vmem_limit_bytes=min(4 * held + (4 << 20), 56 << 20))


def packed_rows(rank_pad):
    return rank_pad + rank_pad // 2


def lengthen(x, size):
    return jnp.concatenate([x, jnp.zeros((size - x.shape[0], x.shape[1]), x.dtype)], axis=0)


def scalar(ref, row, column):
    return ref[row : row + 1, column : column + 1][0, 0]


def stay(x):
    return pltpu.with_memory_space_constraint(x, pltpu.HBM)


def blocks_kernel(
    group,
    order_hbm,
    ranks_hbm,
    latent_hbm,
    v_hbm,
    out_ref,
    order_out,
    ranks_out,
    held_ref,
    order_ref,
    ranks_ref,
    latent_ref,
    v_ref,
    sems,
):
    local, rows, rank_pad, cells = v_ref.shape
    width = latent_ref.shape[1]
    small = [
        pltpu.make_async_copy(order_hbm, order_ref, sems.at[2 * local]),
        pltpu.make_async_copy(ranks_hbm, ranks_ref, sems.at[2 * local + 1]),
    ]
    later = [
        pltpu.make_async_copy(order_hbm, order_out, sems.at[2 * local + 2]),
        pltpu.make_async_copy(ranks_hbm, ranks_out, sems.at[2 * local + 3]),
    ]
    tiles = []
    for j in range(local):
        here = pl.ds(j * cells, cells)
        tiles.append(
            (
                pltpu.make_async_copy(v_hbm.at[:, j], v_ref.at[j], sems.at[2 * j]),
                pltpu.make_async_copy(latent_hbm.at[here], latent_ref.at[here], sems.at[2 * j + 1]),
            )
        )
    for copies in tiles:
        for copy in copies:
            copy.start()
    for copy in small + later:
        copy.start()
    for j in range(local):
        for copy in tiles[j]:
            copy.wait()

        def some(g):
            v_rows = v_ref[j, pl.ds(g * group, group)].reshape(group * rank_pad, cells)
            made = product(v_rows, latent_ref[j * cells : (j + 1) * cells, :])
            held_ref[j, pl.ds(g * group, group)] = made.reshape(group, rank_pad, width)

        repeat(rows // group, some)
    for copy in small:
        copy.wait()
    rank_index = lax.broadcasted_iota(jnp.int32, (rank_pad, width), 0)
    size = packed_rows(rank_pad)

    def place(g):
        for i in range(group):
            c = g * group + i
            q = order_ref[0, c]
            for pair in range(local // 2):
                left, right = 2 * pair, 2 * pair + 1
                cut = ranks_ref[left, q]
                first = jnp.where(rank_index < cut, held_ref[left, q], 0.0)
                second = jnp.where(rank_index < ranks_ref[right, q], held_ref[right, q], 0.0)
                base = pair * (size + MARK)
                out_ref[c, base : base + size, :] = lengthen(first, size) + pltpu.roll(lengthen(second, size), cut, 0)
                out_ref[c, base + size : base + size + MARK, :] = jnp.full((MARK, width), cut.astype(F32))

    repeat(rows // group, place)
    for copy in later:
        copy.wait()


def owner_kernel(
    chunk,
    rank_pad,
    wells_hbm,
    received_ref,
    u_ref,
    observed_ref,
    field_hbm,
    packed_ref,
    stacked_ref,
    field_ref,
    at_wells_ref,
    rows_ref,
    wells_ref,
    sem,
    field_sem,
):
    sources = received_ref.shape[0]
    depth, width = stacked_ref.shape
    wells = observed_ref.shape[0]
    size = packed_rows(rank_pad)
    pairs = received_ref.shape[1] // (size + MARK)
    copy = pltpu.make_async_copy(wells_hbm, wells_ref, sem)
    copy.start()
    rank_index = lax.broadcasted_iota(jnp.int32, (rank_pad, width), 0)
    packed_index = lax.broadcasted_iota(jnp.int32, (size, width), 0)

    def first_rank(c, pair):
        at = pair * (size + MARK) + size
        return scalar(received_ref.at[c], at, 0).astype(jnp.int32)

    def unpack(c):
        for pair in range(pairs):
            cut = first_rank(c, pair)
            both = received_ref[c, pair * (size + MARK) : pair * (size + MARK) + size, :]
            left = pl.multiple_of((c * pairs + pair) * 2 * rank_pad, 8)
            stacked_ref[pl.ds(left, rank_pad), :] = jnp.where(rank_index < cut, both[:rank_pad], 0.0)
            second = pltpu.roll(both, size - cut, 0)[:rank_pad]
            right = pl.multiple_of(left + rank_pad, 8)
            stacked_ref[pl.ds(right, rank_pad), :] = jnp.where(rank_index < size - cut, second, 0.0)

    def pack(c):
        for pair in range(pairs):
            cut = first_rank(c, pair)
            left = pl.multiple_of((c * pairs + pair) * 2 * rank_pad, 8)
            first = lengthen(stacked_ref[pl.ds(left, rank_pad), :], size)
            right = pl.multiple_of(left + rank_pad, 8)
            second = pltpu.roll(lengthen(stacked_ref[pl.ds(right, rank_pad), :], size), cut, 0)
            packed_ref[c, pair * size : (pair + 1) * size, :] = jnp.where(packed_index < cut, first, second)

    each(sources, unpack)

    def first(k):
        part = product(u_ref[:, pl.ds(k * chunk, chunk)], stacked_ref[pl.ds(k * chunk, chunk), :])
        if depth == chunk:
            field_ref[...] = part
        else:

            @pl.when(k == 0)
            def _():
                field_ref[...] = part

            @pl.when(k > 0)
            def _():
                field_ref[...] += part

    repeat(depth // chunk, first)
    away = pltpu.make_async_copy(field_ref, field_hbm, field_sem)
    away.start()
    copy.wait()
    for w in range(wells):
        cell = wells_ref[0, w]
        at_wells_ref[w : w + 1, :] = field_ref[pl.ds(cell, 1), :]
        rows_ref[w : w + 1, :] = u_ref[pl.ds(cell, 1), :]
    expo = jnp.exp(at_wells_ref[...])
    weighted = (expo - observed_ref[...]) * expo / 0.25

    def back(k):
        stacked_ref[pl.ds(k * chunk, chunk), :] = product(rows_ref[:, pl.ds(k * chunk, chunk)], weighted, (0, 0))

    repeat(depth // chunk, back)
    each(sources, pack)
    away.wait()


def gradient_kernel(
    group, axis, turn, order_ref, ranks_ref, returned_ref, v_ref, latent_ref, *refs
):
    out_refs, (ordered_ref, total_ref) = refs[:-2], refs[-2:]
    rows, local, rank_pad, cells = v_ref.shape
    width = latent_ref.shape[1]
    rank_index = lax.broadcasted_iota(jnp.int32, (rank_pad, width), 0)

    packed = packed_rows(rank_pad)

    square = (rows, rows)
    is_owner = order_ref[...] == lax.broadcasted_iota(jnp.int32, square, 0)
    owners = jnp.sum(jnp.where(is_owner, lax.broadcasted_iota(jnp.int32, square, 1), 0), axis=1, keepdims=True)

    def place():
        for q in range(rows):
            c = owners[q : q + 1, :][0, 0]
            for pair in range(local // 2):
                left, right = 2 * pair, 2 * pair + 1
                cut = scalar(ranks_ref, left, q)
                both = returned_ref[c, pair * packed : (pair + 1) * packed, :]
                ordered_ref[left, q] = jnp.where(rank_index < cut, both[:rank_pad], 0.0)
                second = pltpu.roll(both, packed - cut, 0)[:rank_pad]
                ordered_ref[right, q] = jnp.where(rank_index < scalar(ranks_ref, right, q), second, 0.0)

    place()

    def some(g):
        for j in range(local):
            v_rows = v_ref[pl.ds(g * group, group), j].reshape(group * rank_pad, cells)
            part = product(v_rows, ordered_ref[j, pl.ds(g * group, group)].reshape(group * rank_pad, width), (0, 0))
            here = slice(j * cells, (j + 1) * cells)
            if rows == group:
                total_ref[here, :] = part
            else:

                @pl.when(g == 0)
                def _():
                    total_ref[here, :] = part

                @pl.when(g > 0)
                def _():
                    total_ref[here, :] += part

    repeat(rows // group, some)
    me = lax.axis_index(axis)
    size = out_refs[0].shape[0]
    for step, out_ref in enumerate(out_refs):
        there = pl.ds(pl.multiple_of(turn(me, step) * size, size), size)
        if step == 0:
            out_ref[...] = total_ref[there, :] + latent_ref[there, :]
        else:
            out_ref[...] = total_ref[there, :]


def on_device(n_row, latent, v_basis, u_basis, ranks, slot_row, wells, observed):
    rows, _, local, rank_pad, cells = v_basis.shape
    width = latent.shape[1]
    v_rows = v_basis[:, 0]
    u_owned = u_basis[0, 0]
    observed_here = observed[0, 0]
    well_count = observed_here.shape[0]
    pairs, packed = local // 2, packed_rows(rank_pad)
    depth = u_owned.shape[1]
    group = 8 if rows % 8 == 0 else 1
    chunk = 768 if depth % 768 == 0 else depth
    sent, order_here, ranks_here = pl.pallas_call(
        functools.partial(blocks_kernel, group),
        out_shape=(
            jax.ShapeDtypeStruct((rows, pairs * (packed + MARK), width), F32),
            jax.ShapeDtypeStruct((1, rows), jnp.int32),
            jax.ShapeDtypeStruct((local, rows), jnp.int32),
        ),
        in_specs=[HBM] * 4,
        out_specs=(VMEM,) * 3,
        scratch_shapes=[
            pltpu.VMEM((local, rows, rank_pad, width), F32),
            pltpu.SMEM(slot_row.shape, jnp.int32),
            pltpu.SMEM((local, rows), jnp.int32),
            pltpu.VMEM(latent.shape, F32),
            pltpu.VMEM((local, rows, rank_pad, cells), F32),
            pltpu.SemaphoreType.DMA((2 * local + 4,)),
        ],
        compiler_params=params([latent, v_rows]),
        name="blocks",
    )(stay(slot_row), stay(ranks[:, 0].T), stay(latent), stay(v_rows))
    received = lax.all_to_all(sent, "col", split_axis=0, concat_axis=0, tiled=True)
    field, adjoint = pl.pallas_call(
        functools.partial(owner_kernel, chunk, rank_pad),
        out_shape=(
            jax.ShapeDtypeStruct((cells, width), F32),
            jax.ShapeDtypeStruct((rows, pairs * packed, width), F32),
        ),
        in_specs=[HBM, VMEM, VMEM, VMEM],
        out_specs=(HBM, VMEM),
        scratch_shapes=[
            pltpu.VMEM((depth, width), F32),
            pltpu.VMEM((cells, width), F32),
            pltpu.VMEM((well_count, width), F32),
            pltpu.VMEM((well_count, depth), F32),
            pltpu.SMEM((1, well_count), jnp.int32),
            pltpu.SemaphoreType.DMA,
            pltpu.SemaphoreType.DMA,
        ],
        compiler_params=params([received, u_owned, observed_here]),
        name="owner",
    )(stay(wells[0]), received, u_owned, observed_here)
    returned = lax.all_to_all(adjoint, "col", split_axis=0, concat_axis=0, tiled=True)
    paired = n_row & (n_row - 1) == 0

    def turn(index, step):
        return index ^ step if paired else lax.rem(index + step, n_row)

    size = local * cells // n_row
    parts = pl.pallas_call(
        functools.partial(gradient_kernel, group, "row", turn),
        out_shape=[jax.ShapeDtypeStruct((size, width), F32)] * n_row,
        in_specs=[VMEM] * 5,
        out_specs=[VMEM] * n_row,
        scratch_shapes=[pltpu.VMEM((local, rows, rank_pad, width), F32), pltpu.VMEM((local * cells, width), F32)],
        compiler_params=params([returned, v_rows, latent]),
        name="gradient",
    )(order_here, ranks_here, returned, v_rows, latent)
    gradient = parts[0]
    for step in range(1, n_row):
        pairs = [(i, i ^ step if paired else (i + step) % n_row) for i in range(n_row)]
        gradient = gradient + lax.ppermute(parts[step], "row", pairs)
    return field[None, None], gradient


def solution(mesh):
    placed = (
        P("col", None),
        P(None, "row", "col", None, None),
        P("col", "row", None, None),
        P(None, "row", "col"),
        P("row", None),
        P("col", "row", None),
        P("col", "row", None, None),
    )
    return jax.shard_map(
        functools.partial(on_device, mesh.shape["row"]),
        mesh=mesh,
        in_specs=placed,
        out_specs=(P("col", "row", None, None), P(("col", "row"), None)),
        check_vma=False,
    )
```

```python
import functools

import jax
import jax.numpy as jnp
from jax import lax
from jax.experimental import pallas as pl
from jax.experimental.pallas import tpu as pltpu
from jax.sharding import PartitionSpec as P

F32 = jnp.float32
BF16 = jnp.bfloat16
VMEM = pl.BlockSpec(memory_space=pltpu.VMEM)
HBM = pl.BlockSpec(memory_space=pltpu.HBM)
MARK = 8


def split_rest(x):
    high = x.astype(BF16)
    return high, x - high.astype(F32)


def split(x):
    high, rest = split_rest(x)
    return high, rest.astype(BF16)


def product(a, b, contract=(1, 0)):
    return product_of(*split(a), b, contract)


def product_of(a_high, a_low, b, contract=(1, 0)):
    dims = (((contract[0],), (contract[1],)), ((), ()))
    b_high, b_low = split(b)
    both = lax.dot_general(a_high, jnp.concatenate([b_high, b_low], axis=1), dims, preferred_element_type=F32)
    width = b.shape[1]
    return both[:, :width] + both[:, width:] + lax.dot_general(a_low, b_high, dims, preferred_element_type=F32)


def repeat(count, body):
    if count == 1:
        body(0)
    else:
        pl.loop(0, count)(body)


def each(count, body):
    if count <= 16:
        for i in range(count):
            body(i)
    else:
        pl.loop(0, count)(body)


def params(arrays):
    held = sum(a.size * a.dtype.itemsize for a in arrays)
    return pltpu.CompilerParams(vmem_limit_bytes=min(4 * held + (4 << 20), 56 << 20))


def packed_rows(rank_pad):
    return rank_pad + rank_pad // 2


def lengthen(x, size):
    return jnp.concatenate([x, jnp.zeros((size - x.shape[0], x.shape[1]), x.dtype)], axis=0)


def scalar(ref, row, column):
    return ref[row : row + 1, column : column + 1][0, 0]


def stay(x):
    return pltpu.with_memory_space_constraint(x, pltpu.HBM)


def blocks_kernel(
    group,
    order_hbm,
    ranks_hbm,
    wells_hbm,
    latent_hbm,
    v_hbm,
    out_ref,
    order_out,
    ranks_out,
    wells_out,
    held_ref,
    order_ref,
    ranks_ref,
    latent_ref,
    v_ref,
    sems,
):
    local, rows, rank_pad, cells = v_ref.shape
    width = latent_ref.shape[1]
    small = [
        pltpu.make_async_copy(order_hbm, order_ref, sems.at[2 * local]),
        pltpu.make_async_copy(ranks_hbm, ranks_ref, sems.at[2 * local + 1]),
    ]
    later = [
        pltpu.make_async_copy(order_hbm, order_out, sems.at[2 * local + 2]),
        pltpu.make_async_copy(ranks_hbm, ranks_out, sems.at[2 * local + 3]),
        pltpu.make_async_copy(wells_hbm, wells_out, sems.at[2 * local + 4]),
    ]
    tiles = []
    for j in range(local):
        here = pl.ds(j * cells, cells)
        tiles.append(
            (
                pltpu.make_async_copy(v_hbm.at[:, j], v_ref.at[j], sems.at[2 * j]),
                pltpu.make_async_copy(latent_hbm.at[here], latent_ref.at[here], sems.at[2 * j + 1]),
            )
        )
    for copies in tiles:
        for copy in copies:
            copy.start()
    for copy in small + later:
        copy.start()
    for j in range(local):
        for copy in tiles[j]:
            copy.wait()

        def some(g):
            v_rows = v_ref[j, pl.ds(g * group, group)].reshape(group * rank_pad, cells)
            made = product(v_rows, latent_ref[j * cells : (j + 1) * cells, :])
            held_ref[j, pl.ds(g * group, group)] = made.reshape(group, rank_pad, width)

        repeat(rows // group, some)
    for copy in small:
        copy.wait()
    rank_index = lax.broadcasted_iota(jnp.int32, (rank_pad, width), 0)
    size = packed_rows(rank_pad)

    def place(g):
        for i in range(group):
            c = g * group + i
            q = order_ref[0, c]
            for pair in range(local // 2):
                left, right = 2 * pair, 2 * pair + 1
                cut = ranks_ref[left, q]
                first = jnp.where(rank_index < cut, held_ref[left, q], 0.0)
                second = jnp.where(rank_index < ranks_ref[right, q], held_ref[right, q], 0.0)
                base = pair * (size + MARK)
                out_ref[c, base : base + size, :] = lengthen(first, size) + pltpu.roll(lengthen(second, size), cut, 0)
                out_ref[c, base + size : base + size + MARK, :] = jnp.full((MARK, width), cut.astype(F32))

    repeat(rows // group, place)
    for copy in later:
        copy.wait()


def owner_kernel(
    chunk,
    rank_pad,
    wells_ref,
    received_ref,
    u_ref,
    observed_ref,
    field_ref,
    packed_ref,
    stacked_ref,
    rows_ref,
):
    sources = received_ref.shape[0]
    depth, width = stacked_ref.shape
    wells = observed_ref.shape[0]
    cells = u_ref.shape[0]
    size = packed_rows(rank_pad)
    pairs = received_ref.shape[1] // (size + MARK)
    rank_index = lax.broadcasted_iota(jnp.int32, (rank_pad, width), 0)
    packed_index = lax.broadcasted_iota(jnp.int32, (size, width), 0)

    def first_rank(c, pair):
        at = pair * (size + MARK) + size
        return scalar(received_ref.at[c], at, 0).astype(jnp.int32)

    def unpack(c):
        for pair in range(pairs):
            cut = first_rank(c, pair)
            both = received_ref[c, pair * (size + MARK) : pair * (size + MARK) + size, :]
            left = pl.multiple_of((c * pairs + pair) * 2 * rank_pad, 8)
            stacked_ref[pl.ds(left, rank_pad), :] = jnp.where(rank_index < cut, both[:rank_pad], 0.0)
            second = pltpu.roll(both, size - cut, 0)[:rank_pad]
            right = pl.multiple_of(left + rank_pad, 8)
            stacked_ref[pl.ds(right, rank_pad), :] = jnp.where(rank_index < size - cut, second, 0.0)

    def pack(c):
        for pair in range(pairs):
            cut = first_rank(c, pair)
            left = pl.multiple_of((c * pairs + pair) * 2 * rank_pad, 8)
            first = lengthen(stacked_ref[pl.ds(left, rank_pad), :], size)
            right = pl.multiple_of(left + rank_pad, 8)
            second = pltpu.roll(lengthen(stacked_ref[pl.ds(right, rank_pad), :], size), cut, 0)
            packed_ref[c, pair * size : (pair + 1) * size, :] = jnp.where(packed_index < cut, first, second)

    each(sources, unpack)
    picked = jnp.where(lax.broadcasted_iota(jnp.int32, (cells, wells), 0) == wells_ref[...], 1.0, 0.0).astype(BF16)
    turned = (((0,), (0,)), ((), ()))

    def first(k):
        here = pl.ds(k * chunk, chunk)
        high, low = split(u_ref[:, here])
        part = product_of(high, low, stacked_ref[here, :])
        own = lax.dot_general(picked, high, turned, preferred_element_type=F32).astype(BF16)
        rows_ref[0:wells, here] = own
        rows_ref[wells : 2 * wells, here] = own
        rows_ref[2 * wells :, here] = lax.dot_general(picked, low, turned, preferred_element_type=F32).astype(BF16)
        if depth == chunk:
            field_ref[...] = part
        else:

            @pl.when(k == 0)
            def _():
                field_ref[...] = part

            @pl.when(k > 0)
            def _():
                field_ref[...] += part

    repeat(depth // chunk, first)
    high, rest = split_rest(field_ref[...])
    middle, rest = split_rest(rest)
    parts = jnp.concatenate([high, middle, rest.astype(BF16)], axis=1)
    parts = lax.dot_general(picked, parts, turned, preferred_element_type=F32)
    expo = jnp.exp(parts[:, :width] + parts[:, width : 2 * width] + parts[:, 2 * width :])
    weighted = (expo - observed_ref[...]) * expo / 0.25
    high, low = split(weighted)
    below = jnp.concatenate([high, low, high], axis=0)

    def back(k):
        here = pl.ds(k * chunk, chunk)
        stacked_ref[here, :] = lax.dot_general(rows_ref[:, here], below, turned, preferred_element_type=F32)

    repeat(depth // chunk, back)
    each(sources, pack)


def gradient_kernel(
    group, axis, turn, order_ref, ranks_ref, returned_ref, v_ref, latent_ref, *refs
):
    out_refs, (ordered_ref, total_ref) = refs[:-2], refs[-2:]
    rows, local, rank_pad, cells = v_ref.shape
    width = latent_ref.shape[1]
    rank_index = lax.broadcasted_iota(jnp.int32, (rank_pad, width), 0)

    packed = packed_rows(rank_pad)

    square = (rows, rows)
    is_owner = order_ref[...] == lax.broadcasted_iota(jnp.int32, square, 0)
    owners = jnp.sum(jnp.where(is_owner, lax.broadcasted_iota(jnp.int32, square, 1), 0), axis=1, keepdims=True)

    def place():
        for q in range(rows):
            c = owners[q : q + 1, :][0, 0]
            for pair in range(local // 2):
                left, right = 2 * pair, 2 * pair + 1
                cut = scalar(ranks_ref, left, q)
                both = returned_ref[c, pair * packed : (pair + 1) * packed, :]
                ordered_ref[left, q] = jnp.where(rank_index < cut, both[:rank_pad], 0.0)
                second = pltpu.roll(both, packed - cut, 0)[:rank_pad]
                ordered_ref[right, q] = jnp.where(rank_index < scalar(ranks_ref, right, q), second, 0.0)

    place()

    def some(g):
        for j in range(local):
            v_rows = v_ref[pl.ds(g * group, group), j].reshape(group * rank_pad, cells)
            part = product(v_rows, ordered_ref[j, pl.ds(g * group, group)].reshape(group * rank_pad, width), (0, 0))
            here = slice(j * cells, (j + 1) * cells)
            if rows == group:
                total_ref[here, :] = part
            else:

                @pl.when(g == 0)
                def _():
                    total_ref[here, :] = part

                @pl.when(g > 0)
                def _():
                    total_ref[here, :] += part

    repeat(rows // group, some)
    me = lax.axis_index(axis)
    size = out_refs[0].shape[0]
    for step, out_ref in enumerate(out_refs):
        there = pl.ds(pl.multiple_of(turn(me, step) * size, size), size)
        if step == 0:
            out_ref[...] = total_ref[there, :] + latent_ref[there, :]
        else:
            out_ref[...] = total_ref[there, :]


def on_device(n_row, latent, v_basis, u_basis, ranks, slot_row, wells, observed):
    rows, _, local, rank_pad, cells = v_basis.shape
    width = latent.shape[1]
    v_rows = v_basis[:, 0]
    u_owned = u_basis[0, 0]
    observed_here = observed[0, 0]
    well_count = observed_here.shape[0]
    pairs, packed = local // 2, packed_rows(rank_pad)
    depth = u_owned.shape[1]
    group = 8 if rows % 8 == 0 else 1
    chunk = 768 if depth % 768 == 0 else depth
    sent, order_here, ranks_here, wells_here = pl.pallas_call(
        functools.partial(blocks_kernel, group),
        out_shape=(
            jax.ShapeDtypeStruct((rows, pairs * (packed + MARK), width), F32),
            jax.ShapeDtypeStruct((1, rows), jnp.int32),
            jax.ShapeDtypeStruct((local, rows), jnp.int32),
            jax.ShapeDtypeStruct((1, well_count), jnp.int32),
        ),
        in_specs=[HBM] * 5,
        out_specs=(VMEM,) * 4,
        scratch_shapes=[
            pltpu.VMEM((local, rows, rank_pad, width), F32),
            pltpu.SMEM(slot_row.shape, jnp.int32),
            pltpu.SMEM((local, rows), jnp.int32),
            pltpu.VMEM(latent.shape, F32),
            pltpu.VMEM((local, rows, rank_pad, cells), F32),
            pltpu.SemaphoreType.DMA((2 * local + 5,)),
        ],
        compiler_params=params([latent, v_rows]),
        name="blocks",
    )(stay(slot_row), stay(ranks[:, 0].T), stay(wells[0]), stay(latent), stay(v_rows))
    received = lax.all_to_all(sent, "col", split_axis=0, concat_axis=0, tiled=True)
    field, adjoint = pl.pallas_call(
        functools.partial(owner_kernel, chunk, rank_pad),
        out_shape=(
            pltpu.VMEM((cells, width), F32),
            jax.ShapeDtypeStruct((rows, pairs * packed, width), F32),
        ),
        in_specs=[VMEM, VMEM, VMEM, VMEM],
        out_specs=(VMEM, VMEM),
        scratch_shapes=[
            pltpu.VMEM((depth, width), F32),
            pltpu.VMEM((3 * well_count, depth), BF16),
        ],
        compiler_params=params([received, u_owned, observed_here]),
        name="owner",
    )(wells_here, received, u_owned, observed_here)
    returned = lax.all_to_all(adjoint, "col", split_axis=0, concat_axis=0, tiled=True)
    paired = n_row & (n_row - 1) == 0

    def turn(index, step):
        return index ^ step if paired else lax.rem(index + step, n_row)

    size = local * cells // n_row
    parts = pl.pallas_call(
        functools.partial(gradient_kernel, group, "row", turn),
        out_shape=[jax.ShapeDtypeStruct((size, width), F32)] * n_row,
        in_specs=[VMEM] * 5,
        out_specs=[VMEM] * n_row,
        scratch_shapes=[pltpu.VMEM((local, rows, rank_pad, width), F32), pltpu.VMEM((local * cells, width), F32)],
        compiler_params=params([returned, v_rows, latent]),
        name="gradient",
    )(order_here, ranks_here, returned, v_rows, latent)
    gradient = parts[0]
    for step in range(1, n_row):
        pairs = [(i, i ^ step if paired else (i + step) % n_row) for i in range(n_row)]
        gradient = gradient + lax.ppermute(parts[step], "row", pairs)
    return field[None, None], gradient


def solution(mesh):
    placed = (
        P("col", None),
        P(None, "row", "col", None, None),
        P("col", "row", None, None),
        P(None, "row", "col"),
        P("row", None),
        P("col", "row", None),
        P("col", "row", None, None),
    )
    return jax.shard_map(
        functools.partial(on_device, mesh.shape["row"]),
        mesh=mesh,
        in_specs=placed,
        out_specs=(P("col", "row", None, None), P(("col", "row"), None)),
        check_vma=False,
    )
```

```python
import functools

import jax
import jax.numpy as jnp
from jax import lax
from jax.experimental import pallas as pl
from jax.experimental.pallas import tpu as pltpu
from jax.sharding import PartitionSpec as P

F32 = jnp.float32
BF16 = jnp.bfloat16
VMEM = pl.BlockSpec(memory_space=pltpu.VMEM)
HBM = pl.BlockSpec(memory_space=pltpu.HBM)
MARK = 8


def split_rest(x):
    high = x.astype(BF16)
    return high, x - high.astype(F32)


def split(x):
    high, rest = split_rest(x)
    return high, rest.astype(BF16)


def product(a, b, contract=(1, 0)):
    return product_of(*split(a), b, contract)


def product_of(a_high, a_low, b, contract=(1, 0)):
    dims = (((contract[0],), (contract[1],)), ((), ()))
    b_high, b_low = split(b)
    both = lax.dot_general(a_high, jnp.concatenate([b_high, b_low], axis=1), dims, preferred_element_type=F32)
    width = b.shape[1]
    return both[:, :width] + both[:, width:] + lax.dot_general(a_low, b_high, dims, preferred_element_type=F32)


def repeat(count, body):
    if count == 1:
        body(0)
    else:
        pl.loop(0, count)(body)


def each(count, body):
    if count <= 16:
        for i in range(count):
            body(i)
    else:
        pl.loop(0, count)(body)


def params(arrays):
    held = sum(a.size * a.dtype.itemsize for a in arrays)
    return pltpu.CompilerParams(vmem_limit_bytes=min(4 * held + (4 << 20), 56 << 20))


def packed_rows(rank_pad):
    return rank_pad + rank_pad // 2


def lengthen(x, size):
    return jnp.concatenate([x, jnp.zeros((size - x.shape[0], x.shape[1]), x.dtype)], axis=0)


def scalar(ref, row, column):
    return ref[pl.ds(row, 1), column : column + 1][0, 0]


def block(refs, k):
    return refs[k] if len(refs) > 1 else refs[0].at[k]


def partner(refs, k):
    return lax.axis_index("col") ^ k if len(refs) > 1 else k


def stay(x):
    return pltpu.with_memory_space_constraint(x, pltpu.HBM)


def blocks_kernel(group, order_hbm, ranks_hbm, wells_hbm, latent_hbm, v_hbm, *refs):
    out_refs, (plan_ref, wells_out, held_ref, order_ref, ranks_ref, latent_ref, v_ref, sems) = refs[:-8], refs[-8:]
    local, rows, rank_pad, cells = v_ref.shape
    width = latent_ref.shape[1]
    small = [
        pltpu.make_async_copy(order_hbm, order_ref, sems.at[2 * local]),
        pltpu.make_async_copy(ranks_hbm, ranks_ref, sems.at[2 * local + 1]),
    ]
    later = [pltpu.make_async_copy(wells_hbm, wells_out, sems.at[2 * local + 2])]
    tiles = []
    for j in range(local):
        here = pl.ds(j * cells, cells)
        tiles.append(
            (
                pltpu.make_async_copy(v_hbm.at[:, j], v_ref.at[j], sems.at[2 * j]),
                pltpu.make_async_copy(latent_hbm.at[here], latent_ref.at[here], sems.at[2 * j + 1]),
            )
        )
    for copies in tiles:
        for copy in copies:
            copy.start()
    for copy in small + later:
        copy.start()
    for j in range(local):
        for copy in tiles[j]:
            copy.wait()

        def some(g):
            v_rows = v_ref[j, pl.ds(g * group, group)].reshape(group * rank_pad, cells)
            made = product(v_rows, latent_ref[j * cells : (j + 1) * cells, :])
            held_ref[j, pl.ds(g * group, group)] = made.reshape(group, rank_pad, width)

        repeat(rows // group, some)
    for copy in small:
        copy.wait()
    rank_index = lax.broadcasted_iota(jnp.int32, (rank_pad, width), 0)
    size = packed_rows(rank_pad)

    lane = lax.broadcasted_iota(jnp.int32, (1, plan_ref.shape[1]), 1)

    def place(k):
        q = order_ref[0, partner(out_refs, k)]
        plan = jnp.where(lane == 0, q, 0)
        for j in range(local):
            plan = jnp.where(lane == 1 + j, ranks_ref[j, q], plan)
        plan_ref[pl.ds(k, 1), :] = plan
        out_ref = block(out_refs, k)
        for pair in range(local // 2):
            left, right = 2 * pair, 2 * pair + 1
            cut = ranks_ref[left, q]
            first = jnp.where(rank_index < cut, held_ref[left, q], 0.0)
            second = jnp.where(rank_index < ranks_ref[right, q], held_ref[right, q], 0.0)
            base = pair * (size + MARK)
            out_ref[base : base + size, :] = lengthen(first, size) + pltpu.roll(lengthen(second, size), cut, 0)
            out_ref[base + size : base + size + MARK, :] = jnp.full((MARK, width), cut.astype(F32))

    each(rows, place)
    for copy in later:
        copy.wait()


def owner_kernel(chunk, rank_pad, count, wells_ref, u_ref, observed_ref, *refs):
    received_refs, field_ref, packed_refs, (stacked_ref, rows_ref) = (
        refs[:count],
        refs[count],
        refs[count + 1 : 2 * count + 1],
        refs[2 * count + 1 :],
    )
    depth, width = stacked_ref.shape
    wells = observed_ref.shape[0]
    cells = u_ref.shape[0]
    size = packed_rows(rank_pad)
    sources = depth // (received_refs[0].shape[-2] // (size + MARK) * 2 * rank_pad)
    pairs = depth // (sources * 2 * rank_pad)
    rank_index = lax.broadcasted_iota(jnp.int32, (rank_pad, width), 0)
    packed_index = lax.broadcasted_iota(jnp.int32, (size, width), 0)

    def first_rank(k, pair):
        return scalar(block(received_refs, k), pair * (size + MARK) + size, 0).astype(jnp.int32)

    def places(k, pair):
        left = pl.multiple_of((partner(received_refs, k) * pairs + pair) * 2 * rank_pad, 8)
        return pl.ds(left, rank_pad), pl.ds(pl.multiple_of(left + rank_pad, 8), rank_pad)

    def unpack(k):
        for pair in range(pairs):
            cut = first_rank(k, pair)
            both = block(received_refs, k)[pair * (size + MARK) : pair * (size + MARK) + size, :]
            left, right = places(k, pair)
            stacked_ref[left, :] = jnp.where(rank_index < cut, both[:rank_pad], 0.0)
            second = pltpu.roll(both, size - cut, 0)[:rank_pad]
            stacked_ref[right, :] = jnp.where(rank_index < size - cut, second, 0.0)

    def pack(k):
        for pair in range(pairs):
            cut = first_rank(k, pair)
            left, right = places(k, pair)
            first = lengthen(stacked_ref[left, :], size)
            second = pltpu.roll(lengthen(stacked_ref[right, :], size), cut, 0)
            here = slice(pair * size, (pair + 1) * size)
            block(packed_refs, k)[here, :] = jnp.where(packed_index < cut, first, second)

    each(sources, unpack)
    picked = jnp.where(lax.broadcasted_iota(jnp.int32, (cells, wells), 0) == wells_ref[...], 1.0, 0.0).astype(BF16)
    turned = (((0,), (0,)), ((), ()))

    def first(k):
        here = pl.ds(k * chunk, chunk)
        high, low = split(u_ref[:, here])
        part = product_of(high, low, stacked_ref[here, :])
        own = lax.dot_general(picked, high, turned, preferred_element_type=F32).astype(BF16)
        rows_ref[0:wells, here] = own
        rows_ref[wells : 2 * wells, here] = own
        rows_ref[2 * wells :, here] = lax.dot_general(picked, low, turned, preferred_element_type=F32).astype(BF16)
        if depth == chunk:
            field_ref[...] = part
        else:

            @pl.when(k == 0)
            def _():
                field_ref[...] = part

            @pl.when(k > 0)
            def _():
                field_ref[...] += part

    repeat(depth // chunk, first)
    high, rest = split_rest(field_ref[...])
    middle, rest = split_rest(rest)
    parts = jnp.concatenate([high, middle, rest.astype(BF16)], axis=1)
    parts = lax.dot_general(picked, parts, turned, preferred_element_type=F32)
    expo = jnp.exp(parts[:, :width] + parts[:, width : 2 * width] + parts[:, 2 * width :])
    weighted = (expo - observed_ref[...]) * expo / 0.25
    high, low = split(weighted)
    below = jnp.concatenate([high, low, high], axis=0)

    def back(k):
        here = pl.ds(k * chunk, chunk)
        stacked_ref[here, :] = lax.dot_general(rows_ref[:, here], below, turned, preferred_element_type=F32)

    repeat(depth // chunk, back)
    each(sources, pack)


def gradient_kernel(group, axis, turn, count, plan_ref, v_ref, latent_ref, *refs):
    returned_refs, out_refs, (ordered_ref, total_ref) = refs[:count], refs[count:-2], refs[-2:]
    rows, local, rank_pad, cells = v_ref.shape
    width = latent_ref.shape[1]
    rank_index = lax.broadcasted_iota(jnp.int32, (rank_pad, width), 0)

    packed = packed_rows(rank_pad)

    def place(k):
        q = scalar(plan_ref, k, 0)
        for pair in range(local // 2):
            left, right = 2 * pair, 2 * pair + 1
            cut = scalar(plan_ref, k, 1 + left)
            both = block(returned_refs, k)[pair * packed : (pair + 1) * packed, :]
            ordered_ref[left, q] = jnp.where(rank_index < cut, both[:rank_pad], 0.0)
            second = pltpu.roll(both, packed - cut, 0)[:rank_pad]
            ordered_ref[right, q] = jnp.where(rank_index < scalar(plan_ref, k, 1 + right), second, 0.0)

    each(rows, place)

    def some(g):
        for j in range(local):
            v_rows = v_ref[pl.ds(g * group, group), j].reshape(group * rank_pad, cells)
            part = product(v_rows, ordered_ref[j, pl.ds(g * group, group)].reshape(group * rank_pad, width), (0, 0))
            here = slice(j * cells, (j + 1) * cells)
            if rows == group:
                total_ref[here, :] = part
            else:

                @pl.when(g == 0)
                def _():
                    total_ref[here, :] = part

                @pl.when(g > 0)
                def _():
                    total_ref[here, :] += part

    repeat(rows // group, some)
    me = lax.axis_index(axis)
    size = out_refs[0].shape[0]
    for step, out_ref in enumerate(out_refs):
        there = pl.ds(pl.multiple_of(turn(me, step) * size, size), size)
        if step == 0:
            out_ref[...] = total_ref[there, :] + latent_ref[there, :]
        else:
            out_ref[...] = total_ref[there, :]


def exchange(arrays):
    if len(arrays) == 1:
        return [lax.all_to_all(arrays[0], "col", split_axis=0, concat_axis=0, tiled=True)]
    count = len(arrays)
    return [arrays[0]] + [lax.ppermute(arrays[k], "col", [(i, i ^ k) for i in range(count)]) for k in range(1, count)]


def on_device(n_row, latent, v_basis, u_basis, ranks, slot_row, wells, observed):
    rows, _, local, rank_pad, cells = v_basis.shape
    width = latent.shape[1]
    v_rows = v_basis[:, 0]
    u_owned = u_basis[0, 0]
    observed_here = observed[0, 0]
    well_count = observed_here.shape[0]
    pairs, packed = local // 2, packed_rows(rank_pad)
    depth = u_owned.shape[1]
    group = 8 if rows % 8 == 0 else 1
    chunk = 768 if depth % 768 == 0 else depth
    direct = rows <= 8 and rows & (rows - 1) == 0 and rows > 1
    count = rows if direct else 1
    far = [0] + sorted(range(1, count), key=lambda k: (-k.bit_length(), -(k & 1), -k))

    def carried(size):
        shape = (size, width) if direct else (rows, size, width)
        return [jax.ShapeDtypeStruct(shape, F32)] * count

    def sorted_refs(kernel, before, lists):
        def run(*refs):
            refs = list(refs)
            for start in (before + at for at in lists):
                moved = refs[start : start + count]
                refs[start : start + count] = [moved[far.index(k)] for k in range(count)]
            kernel(*refs)

        return run

    outs = pl.pallas_call(
        functools.partial(blocks_kernel, group),
        out_shape=(
            *carried(pairs * (packed + MARK)),
            jax.ShapeDtypeStruct((rows, 128), jnp.int32),
            jax.ShapeDtypeStruct((1, well_count), jnp.int32),
        ),
        in_specs=[HBM] * 5,
        out_specs=(VMEM,) * (count + 2),
        scratch_shapes=[
            pltpu.VMEM((local, rows, rank_pad, width), F32),
            pltpu.SMEM(slot_row.shape, jnp.int32),
            pltpu.SMEM((local, rows), jnp.int32),
            pltpu.VMEM(latent.shape, F32),
            pltpu.VMEM((local, rows, rank_pad, cells), F32),
            pltpu.SemaphoreType.DMA((2 * local + 3,)),
        ],
        compiler_params=params([latent, v_rows]),
        name="blocks",
    )(stay(slot_row), stay(ranks[:, 0].T), stay(wells[0]), stay(latent), stay(v_rows))
    sent, (plan, wells_here) = outs[:count], outs[count:]
    received = exchange(sent)
    field, *adjoint = pl.pallas_call(
        sorted_refs(functools.partial(owner_kernel, chunk, rank_pad, count), 3, [0]),
        out_shape=(pltpu.VMEM((cells, width), F32), *carried(pairs * packed)),
        in_specs=[VMEM] * (3 + count),
        out_specs=(VMEM,) * (1 + count),
        scratch_shapes=[pltpu.VMEM((depth, width), F32), pltpu.VMEM((3 * well_count, depth), BF16)],
        compiler_params=params([u_owned, u_owned, observed_here]),
        name="owner",
    )(wells_here, u_owned, observed_here, *[received[k] for k in far])
    returned = exchange(adjoint)
    paired = n_row & (n_row - 1) == 0

    def turn(index, step):
        return index ^ step if paired else lax.rem(index + step, n_row)

    size = local * cells // n_row
    parts = pl.pallas_call(
        sorted_refs(functools.partial(gradient_kernel, group, "row", turn, count), 3, [0]),
        out_shape=[jax.ShapeDtypeStruct((size, width), F32)] * n_row,
        in_specs=[VMEM] * (3 + count),
        out_specs=[VMEM] * n_row,
        scratch_shapes=[pltpu.VMEM((local, rows, rank_pad, width), F32), pltpu.VMEM((local * cells, width), F32)],
        compiler_params=params([u_owned, v_rows, latent]),
        name="gradient",
    )(plan, v_rows, latent, *[returned[k] for k in far])
    gradient = parts[0]
    for step in range(1, n_row):
        pairs_of = [(i, i ^ step if paired else (i + step) % n_row) for i in range(n_row)]
        gradient = gradient + lax.ppermute(parts[step], "row", pairs_of)
    return field[None, None], gradient


def solution(mesh):
    placed = (
        P("col", None),
        P(None, "row", "col", None, None),
        P("col", "row", None, None),
        P(None, "row", "col"),
        P("row", None),
        P("col", "row", None),
        P("col", "row", None, None),
    )
    return jax.shard_map(
        functools.partial(on_device, mesh.shape["row"]),
        mesh=mesh,
        in_specs=placed,
        out_specs=(P("col", "row", None, None), P(("col", "row"), None)),
        check_vma=False,
    )
```

```python
import functools

import jax
import jax.numpy as jnp
from jax import lax
from jax.experimental import pallas as pl
from jax.experimental.pallas import tpu as pltpu
from jax.sharding import PartitionSpec as P

F32 = jnp.float32
BF16 = jnp.bfloat16
VMEM = pl.BlockSpec(memory_space=pltpu.VMEM)
HBM = pl.BlockSpec(memory_space=pltpu.HBM)
MARK = 8


def split_rest(x):
    high = x.astype(BF16)
    return high, x - high.astype(F32)


def split(x):
    high, rest = split_rest(x)
    return high, rest.astype(BF16)


def product(a, b, contract=(1, 0)):
    return product_of(*split(a), b, contract)


def product_of(a_high, a_low, b, contract=(1, 0)):
    dims = (((contract[0],), (contract[1],)), ((), ()))
    b_high, b_low = split(b)
    both = lax.dot_general(a_high, jnp.concatenate([b_high, b_low], axis=1), dims, preferred_element_type=F32)
    width = b.shape[1]
    return both[:, :width] + both[:, width:] + lax.dot_general(a_low, b_high, dims, preferred_element_type=F32)


def repeat(count, body):
    if count == 1:
        body(0)
    else:
        pl.loop(0, count)(body)


def each(count, body):
    if count <= 16:
        for i in range(count):
            body(i)
    else:
        pl.loop(0, count)(body)


def params(arrays):
    held = sum(a.size * a.dtype.itemsize for a in arrays)
    return pltpu.CompilerParams(vmem_limit_bytes=min(4 * held + (4 << 20), 56 << 20))


def packed_rows(rank_pad):
    return rank_pad + rank_pad // 2


def lengthen(x, size):
    return jnp.concatenate([x, jnp.zeros((size - x.shape[0], x.shape[1]), x.dtype)], axis=0)


def scalar(ref, row, column):
    return ref[pl.ds(row, 1), column : column + 1][0, 0]


def block(refs, k):
    return refs[k] if len(refs) > 1 else refs[0].at[k]


def partner(refs, k):
    return lax.axis_index("col") ^ k if len(refs) > 1 else k


def stay(x):
    return pltpu.with_memory_space_constraint(x, pltpu.HBM)


def blocks_kernel(group, order_hbm, ranks_hbm, wells_hbm, latent_hbm, v_hbm, *refs):
    out_refs, (plan_ref, wells_out, held_ref, order_ref, ranks_ref, latent_ref, v_ref, sems) = refs[:-8], refs[-8:]
    local, rows, rank_pad, cells = v_ref.shape
    width = latent_ref.shape[1]
    small = [
        pltpu.make_async_copy(order_hbm, order_ref, sems.at[2 * local]),
        pltpu.make_async_copy(ranks_hbm, ranks_ref, sems.at[2 * local + 1]),
    ]
    later = [pltpu.make_async_copy(wells_hbm, wells_out, sems.at[2 * local + 2])]
    tiles = []
    for j in range(local):
        here = pl.ds(j * cells, cells)
        tiles.append(
            (
                pltpu.make_async_copy(v_hbm.at[:, j], v_ref.at[j], sems.at[2 * j]),
                pltpu.make_async_copy(latent_hbm.at[here], latent_ref.at[here], sems.at[2 * j + 1]),
            )
        )
    for copies in tiles:
        for copy in copies:
            copy.start()
    for copy in small + later:
        copy.start()
    for j in range(local):
        for copy in tiles[j]:
            copy.wait()

        def some(g):
            v_rows = v_ref[j, pl.ds(g * group, group)].reshape(group * rank_pad, cells)
            made = product(v_rows, latent_ref[j * cells : (j + 1) * cells, :])
            held_ref[j, pl.ds(g * group, group)] = made.reshape(group, rank_pad, width)

        repeat(rows // group, some)
    for copy in small:
        copy.wait()
    rank_index = lax.broadcasted_iota(jnp.int32, (rank_pad, width), 0)
    size = packed_rows(rank_pad)

    lane = lax.broadcasted_iota(jnp.int32, (1, plan_ref.shape[1]), 1)

    def place(k):
        q = order_ref[0, partner(out_refs, k)]
        plan = jnp.where(lane == 0, q, 0)
        for j in range(local):
            plan = jnp.where(lane == 1 + j, ranks_ref[j, q], plan)
        plan_ref[pl.ds(k, 1), :] = plan
        out_ref = block(out_refs, k)
        for pair in range(local // 2):
            left, right = 2 * pair, 2 * pair + 1
            cut = ranks_ref[left, q]
            first = jnp.where(rank_index < cut, held_ref[left, q], 0.0)
            second = jnp.where(rank_index < ranks_ref[right, q], held_ref[right, q], 0.0)
            base = pair * (size + MARK)
            out_ref[base : base + size, :] = lengthen(first, size) + pltpu.roll(lengthen(second, size), cut, 0)
            out_ref[base + size : base + size + MARK, :] = jnp.full((MARK, width), cut.astype(F32))

    each(rows, place)
    for copy in later:
        copy.wait()


def owner_kernel(chunk, rank_pad, count, wells_ref, u_ref, observed_ref, *refs):
    received_refs, field_ref, packed_refs, (stacked_ref, rows_ref) = (
        refs[:count],
        refs[count],
        refs[count + 1 : 2 * count + 1],
        refs[2 * count + 1 :],
    )
    depth, width = stacked_ref.shape
    wells = observed_ref.shape[0]
    cells = u_ref.shape[0]
    size = packed_rows(rank_pad)
    sources = depth // (received_refs[0].shape[-2] // (size + MARK) * 2 * rank_pad)
    pairs = depth // (sources * 2 * rank_pad)
    rank_index = lax.broadcasted_iota(jnp.int32, (rank_pad, width), 0)
    packed_index = lax.broadcasted_iota(jnp.int32, (size, width), 0)

    def first_rank(k, pair):
        return scalar(block(received_refs, k), pair * (size + MARK) + size, 0).astype(jnp.int32)

    def places(k, pair):
        left = pl.multiple_of((partner(received_refs, k) * pairs + pair) * 2 * rank_pad, 8)
        return pl.ds(left, rank_pad), pl.ds(pl.multiple_of(left + rank_pad, 8), rank_pad)

    def unpack(k):
        for pair in range(pairs):
            cut = first_rank(k, pair)
            both = block(received_refs, k)[pair * (size + MARK) : pair * (size + MARK) + size, :]
            left, right = places(k, pair)
            stacked_ref[left, :] = jnp.where(rank_index < cut, both[:rank_pad], 0.0)
            second = pltpu.roll(both, size - cut, 0)[:rank_pad]
            stacked_ref[right, :] = jnp.where(rank_index < size - cut, second, 0.0)

    def pack(k):
        for pair in range(pairs):
            cut = first_rank(k, pair)
            left, right = places(k, pair)
            first = lengthen(stacked_ref[left, :], size)
            second = pltpu.roll(lengthen(stacked_ref[right, :], size), cut, 0)
            here = slice(pair * size, (pair + 1) * size)
            block(packed_refs, k)[here, :] = jnp.where(packed_index < cut, first, second)

    each(sources, unpack)
    picked = jnp.where(lax.broadcasted_iota(jnp.int32, (cells, wells), 0) == wells_ref[...], 1.0, 0.0).astype(BF16)
    turned = (((0,), (0,)), ((), ()))

    def first(k):
        here = pl.ds(k * chunk, chunk)
        high, low = split(u_ref[:, here])
        part = product_of(high, low, stacked_ref[here, :])
        own = lax.dot_general(picked, high, turned, preferred_element_type=F32).astype(BF16)
        rows_ref[0:wells, here] = own
        rows_ref[wells : 2 * wells, here] = own
        rows_ref[2 * wells :, here] = lax.dot_general(picked, low, turned, preferred_element_type=F32).astype(BF16)
        if depth == chunk:
            field_ref[...] = part
        else:

            @pl.when(k == 0)
            def _():
                field_ref[...] = part

            @pl.when(k > 0)
            def _():
                field_ref[...] += part

    repeat(depth // chunk, first)
    high, rest = split_rest(field_ref[...])
    middle, rest = split_rest(rest)
    parts = jnp.concatenate([high, middle, rest.astype(BF16)], axis=1)
    parts = lax.dot_general(picked, parts, turned, preferred_element_type=F32)
    expo = jnp.exp(parts[:, :width] + parts[:, width : 2 * width] + parts[:, 2 * width :])
    weighted = (expo - observed_ref[...]) * expo / 0.25
    high, low = split(weighted)
    below = jnp.concatenate([high, low, high], axis=0)

    def back(k):
        here = pl.ds(k * chunk, chunk)
        stacked_ref[here, :] = lax.dot_general(rows_ref[:, here], below, turned, preferred_element_type=F32)

    repeat(depth // chunk, back)
    each(sources, pack)


def gradient_kernel(group, axis, turn, count, plan_ref, v_ref, latent_ref, *refs):
    returned_refs, out_refs, (ordered_ref, total_ref) = refs[:count], refs[count:-2], refs[-2:]
    rows, local, rank_pad, cells = v_ref.shape
    width = latent_ref.shape[1]
    rank_index = lax.broadcasted_iota(jnp.int32, (rank_pad, width), 0)

    packed = packed_rows(rank_pad)

    def place(k):
        q = scalar(plan_ref, k, 0)
        for pair in range(local // 2):
            left, right = 2 * pair, 2 * pair + 1
            cut = scalar(plan_ref, k, 1 + left)
            both = block(returned_refs, k)[pair * packed : (pair + 1) * packed, :]
            ordered_ref[left, q] = jnp.where(rank_index < cut, both[:rank_pad], 0.0)
            second = pltpu.roll(both, packed - cut, 0)[:rank_pad]
            ordered_ref[right, q] = jnp.where(rank_index < scalar(plan_ref, k, 1 + right), second, 0.0)

    each(rows, place)

    def some(g):
        for j in range(local):
            v_rows = v_ref[pl.ds(g * group, group), j].reshape(group * rank_pad, cells)
            part = product(v_rows, ordered_ref[j, pl.ds(g * group, group)].reshape(group * rank_pad, width), (0, 0))
            here = slice(j * cells, (j + 1) * cells)
            if rows == group:
                total_ref[here, :] = part
            else:

                @pl.when(g == 0)
                def _():
                    total_ref[here, :] = part

                @pl.when(g > 0)
                def _():
                    total_ref[here, :] += part

    repeat(rows // group, some)
    me = lax.axis_index(axis)
    size = out_refs[0].shape[0]
    for step, out_ref in enumerate(out_refs):
        there = pl.ds(pl.multiple_of(turn(me, step) * size, size), size)
        if step == 0:
            out_ref[...] = total_ref[there, :] + latent_ref[there, :]
        else:
            out_ref[...] = total_ref[there, :]


def exchange(arrays):
    if len(arrays) == 1:
        return [lax.all_to_all(arrays[0], "col", split_axis=0, concat_axis=0, tiled=True)]
    count = len(arrays)
    return [arrays[0]] + [lax.ppermute(arrays[k], "col", [(i, i ^ k) for i in range(count)]) for k in range(1, count)]


def on_device(n_row, latent, v_basis, u_basis, ranks, slot_row, wells, observed):
    rows, _, local, rank_pad, cells = v_basis.shape
    width = latent.shape[1]
    v_rows = v_basis[:, 0]
    u_owned = u_basis[0, 0]
    observed_here = observed[0, 0]
    well_count = observed_here.shape[0]
    pairs, packed = local // 2, packed_rows(rank_pad)
    depth = u_owned.shape[1]
    group = 8 if rows % 8 == 0 else 1
    chunk = 768 if depth % 768 == 0 else depth
    direct = rows <= 8 and rows & (rows - 1) == 0 and rows > 1
    count = rows if direct else 1
    far = [0] + sorted(range(1, count), key=lambda k: (-k.bit_length(), (k & 1) ^ (k.bit_length() == 2), k))

    def carried(size):
        shape = (size, width) if direct else (rows, size, width)
        return [jax.ShapeDtypeStruct(shape, F32)] * count

    def sorted_refs(kernel, before, lists):
        def run(*refs):
            refs = list(refs)
            for start in (before + at for at in lists):
                moved = refs[start : start + count]
                refs[start : start + count] = [moved[far.index(k)] for k in range(count)]
            kernel(*refs)

        return run

    outs = pl.pallas_call(
        functools.partial(blocks_kernel, group),
        out_shape=(
            *carried(pairs * (packed + MARK)),
            jax.ShapeDtypeStruct((rows, 128), jnp.int32),
            jax.ShapeDtypeStruct((1, well_count), jnp.int32),
        ),
        in_specs=[HBM] * 5,
        out_specs=(VMEM,) * (count + 2),
        scratch_shapes=[
            pltpu.VMEM((local, rows, rank_pad, width), F32),
            pltpu.SMEM(slot_row.shape, jnp.int32),
            pltpu.SMEM((local, rows), jnp.int32),
            pltpu.VMEM(latent.shape, F32),
            pltpu.VMEM((local, rows, rank_pad, cells), F32),
            pltpu.SemaphoreType.DMA((2 * local + 3,)),
        ],
        compiler_params=params([latent, v_rows]),
        name="blocks",
    )(stay(slot_row), stay(ranks[:, 0].T), stay(wells[0]), stay(latent), stay(v_rows))
    sent, (plan, wells_here) = outs[:count], outs[count:]
    received = exchange(sent)
    field, *adjoint = pl.pallas_call(
        sorted_refs(functools.partial(owner_kernel, chunk, rank_pad, count), 3, [0]),
        out_shape=(pltpu.VMEM((cells, width), F32), *carried(pairs * packed)),
        in_specs=[VMEM] * (3 + count),
        out_specs=(VMEM,) * (1 + count),
        scratch_shapes=[pltpu.VMEM((depth, width), F32), pltpu.VMEM((3 * well_count, depth), BF16)],
        compiler_params=params([u_owned, u_owned, observed_here]),
        name="owner",
    )(wells_here, u_owned, observed_here, *[received[k] for k in far])
    returned = exchange(adjoint)
    paired = n_row & (n_row - 1) == 0

    def turn(index, step):
        return index ^ step if paired else lax.rem(index + step, n_row)

    size = local * cells // n_row
    parts = pl.pallas_call(
        sorted_refs(functools.partial(gradient_kernel, group, "row", turn, count), 3, [0]),
        out_shape=[jax.ShapeDtypeStruct((size, width), F32)] * n_row,
        in_specs=[VMEM] * (3 + count),
        out_specs=[VMEM] * n_row,
        scratch_shapes=[pltpu.VMEM((local, rows, rank_pad, width), F32), pltpu.VMEM((local * cells, width), F32)],
        compiler_params=params([u_owned, v_rows, latent]),
        name="gradient",
    )(plan, v_rows, latent, *[returned[k] for k in far])
    gradient = parts[0]
    for step in range(1, n_row):
        pairs_of = [(i, i ^ step if paired else (i + step) % n_row) for i in range(n_row)]
        gradient = gradient + lax.ppermute(parts[step], "row", pairs_of)
    return field[None, None], gradient


def solution(mesh):
    placed = (
        P("col", None),
        P(None, "row", "col", None, None),
        P("col", "row", None, None),
        P(None, "row", "col"),
        P("row", None),
        P("col", "row", None),
        P("col", "row", None, None),
    )
    return jax.shard_map(
        functools.partial(on_device, mesh.shape["row"]),
        mesh=mesh,
        in_specs=placed,
        out_specs=(P("col", "row", None, None), P(("col", "row"), None)),
        check_vma=False,
    )
```

```python
import functools

import jax
import jax.numpy as jnp
from jax import lax
from jax.experimental import pallas as pl
from jax.experimental.pallas import tpu as pltpu
from jax.sharding import PartitionSpec as P

F32 = jnp.float32
BF16 = jnp.bfloat16
VMEM = pl.BlockSpec(memory_space=pltpu.VMEM)
HBM = pl.BlockSpec(memory_space=pltpu.HBM)
MARK = 8


def split_rest(x):
    high = x.astype(BF16)
    return high, x - high.astype(F32)


def split(x):
    high, rest = split_rest(x)
    return high, rest.astype(BF16)


def product(a, b, contract=(1, 0)):
    return product_of(*split(a), b, contract)


def product_of(a_high, a_low, b, contract=(1, 0)):
    dims = (((contract[0],), (contract[1],)), ((), ()))
    b_high, b_low = split(b)
    both = lax.dot_general(a_high, jnp.concatenate([b_high, b_low], axis=1), dims, preferred_element_type=F32)
    width = b.shape[1]
    return both[:, :width] + both[:, width:] + lax.dot_general(a_low, b_high, dims, preferred_element_type=F32)


def repeat(count, body):
    if count == 1:
        body(0)
    else:
        pl.loop(0, count)(body)


def each(count, body):
    if count <= 16:
        for i in range(count):
            body(i)
    else:
        pl.loop(0, count)(body)


def params(arrays):
    held = sum(a.size * a.dtype.itemsize for a in arrays)
    return pltpu.CompilerParams(vmem_limit_bytes=min(4 * held + (4 << 20), 56 << 20))


def packed_rows(rank_pad):
    return rank_pad + rank_pad // 2


def lengthen(x, size):
    return jnp.concatenate([x, jnp.zeros((size - x.shape[0], x.shape[1]), x.dtype)], axis=0)


def scalar(ref, row, column):
    return ref[pl.ds(row, 1), column : column + 1][0, 0]


def block(refs, k):
    return refs[k] if len(refs) > 1 else refs[0].at[k]


def partner(refs, k):
    return lax.axis_index("col") ^ k if len(refs) > 1 else k


def stay(x):
    return pltpu.with_memory_space_constraint(x, pltpu.HBM)


def blocks_kernel(group, order_hbm, ranks_hbm, wells_hbm, latent_hbm, v_hbm, *refs):
    out_refs, (plan_ref, wells_out, held_ref, order_ref, ranks_ref, latent_ref, v_ref, sems) = refs[:-8], refs[-8:]
    local, rows, rank_pad, cells = v_ref.shape
    width = latent_ref.shape[1]
    small = [
        pltpu.make_async_copy(order_hbm, order_ref, sems.at[2 * local]),
        pltpu.make_async_copy(ranks_hbm, ranks_ref, sems.at[2 * local + 1]),
    ]
    later = [pltpu.make_async_copy(wells_hbm, wells_out, sems.at[2 * local + 2])]
    tiles = []
    for j in range(local):
        here = pl.ds(j * cells, cells)
        tiles.append(
            (
                pltpu.make_async_copy(v_hbm.at[:, j], v_ref.at[j], sems.at[2 * j]),
                pltpu.make_async_copy(latent_hbm.at[here], latent_ref.at[here], sems.at[2 * j + 1]),
            )
        )
    for copies in tiles:
        for copy in copies:
            copy.start()
    for copy in small + later:
        copy.start()
    for j in range(local):
        for copy in tiles[j]:
            copy.wait()

        def some(g):
            v_rows = v_ref[j, pl.ds(g * group, group)].reshape(group * rank_pad, cells)
            made = product(v_rows, latent_ref[j * cells : (j + 1) * cells, :])
            held_ref[j, pl.ds(g * group, group)] = made.reshape(group, rank_pad, width)

        repeat(rows // group, some)
    for copy in small:
        copy.wait()
    rank_index = lax.broadcasted_iota(jnp.int32, (rank_pad, width), 0)
    size = packed_rows(rank_pad)

    lane = lax.broadcasted_iota(jnp.int32, (1, plan_ref.shape[1]), 1)

    def place(k):
        q = order_ref[0, partner(out_refs, k)]
        plan = jnp.where(lane == 0, q, 0)
        for j in range(local):
            plan = jnp.where(lane == 1 + j, ranks_ref[j, q], plan)
        plan_ref[pl.ds(k, 1), :] = plan
        out_ref = block(out_refs, k)
        for pair in range(local // 2):
            left, right = 2 * pair, 2 * pair + 1
            cut = ranks_ref[left, q]
            first = jnp.where(rank_index < cut, held_ref[left, q], 0.0)
            second = jnp.where(rank_index < ranks_ref[right, q], held_ref[right, q], 0.0)
            base = pair * (size + MARK)
            out_ref[base : base + size, :] = lengthen(first, size) + pltpu.roll(lengthen(second, size), cut, 0)
            out_ref[base + size : base + size + MARK, :] = jnp.full((MARK, width), cut.astype(F32))

    each(rows, place)
    for copy in later:
        copy.wait()


def unpack_into(stacked_ref, received_ref, rank_pad, at, pair):
    size = packed_rows(rank_pad)
    width = stacked_ref.shape[1]
    rank_index = lax.broadcasted_iota(jnp.int32, (rank_pad, width), 0)
    base = pair * (size + MARK)
    cut = scalar(received_ref, base + size, 0).astype(jnp.int32)
    both = received_ref[base : base + size, :]
    left = pl.multiple_of(at, 8)
    stacked_ref[pl.ds(left, rank_pad), :] = jnp.where(rank_index < cut, both[:rank_pad], 0.0)
    second = pltpu.roll(both, size - cut, 0)[:rank_pad]
    right = pl.multiple_of(left + rank_pad, 8)
    stacked_ref[pl.ds(right, rank_pad), :] = jnp.where(rank_index < size - cut, second, 0.0)


def half_product(rank_pad, flip, u_ref, received_refs, stacked_ref):
    half = len(received_refs)
    depth = u_ref.shape[1] // 2
    each_rows = depth // half
    me = lax.axis_index("col")
    for k, received_ref in enumerate(received_refs):
        for pair in range(each_rows // (2 * rank_pad)):
            at = ((me ^ k) % half) * each_rows + pair * 2 * rank_pad
            unpack_into(stacked_ref, received_ref, rank_pad, at, pair)
    columns = pl.ds(pl.multiple_of(((me // half) ^ flip) * depth, depth), depth)
    return product(u_ref[:, columns], stacked_ref[:depth, :])


def owner_far_kernel(rank_pad, u_ref, *refs):
    received_refs, (part_ref, stacked_ref) = refs[:-2], refs[-2:]
    part_ref[...] = half_product(rank_pad, 1, u_ref, received_refs, stacked_ref)


def owner_kernel(chunk, rank_pad, count, wells_ref, u_ref, observed_ref, *refs):
    split_up = count > 1
    if split_up:
        far_part_ref, refs = refs[0], refs[1:]
    received_refs, field_ref, packed_refs, (stacked_ref, rows_ref) = (
        refs[:count],
        refs[count],
        refs[count + 1 : 2 * count + 1],
        refs[2 * count + 1 :],
    )
    depth, width = stacked_ref.shape
    wells = observed_ref.shape[0]
    cells = u_ref.shape[0]
    size = packed_rows(rank_pad)
    sources = depth // (received_refs[0].shape[-2] // (size + MARK) * 2 * rank_pad)
    pairs = depth // (sources * 2 * rank_pad)
    rank_index = lax.broadcasted_iota(jnp.int32, (rank_pad, width), 0)
    packed_index = lax.broadcasted_iota(jnp.int32, (size, width), 0)

    def first_rank(k, pair):
        return scalar(block(received_refs, k), pair * (size + MARK) + size, 0).astype(jnp.int32)

    def places(k, pair):
        left = pl.multiple_of((partner(received_refs, k) * pairs + pair) * 2 * rank_pad, 8)
        return pl.ds(left, rank_pad), pl.ds(pl.multiple_of(left + rank_pad, 8), rank_pad)

    def unpack(k):
        for pair in range(pairs):
            cut = first_rank(k, pair)
            both = block(received_refs, k)[pair * (size + MARK) : pair * (size + MARK) + size, :]
            left, right = places(k, pair)
            stacked_ref[left, :] = jnp.where(rank_index < cut, both[:rank_pad], 0.0)
            second = pltpu.roll(both, size - cut, 0)[:rank_pad]
            stacked_ref[right, :] = jnp.where(rank_index < size - cut, second, 0.0)

    def pack(k):
        for pair in range(pairs):
            cut = first_rank(k, pair)
            left, right = places(k, pair)
            first = lengthen(stacked_ref[left, :], size)
            second = pltpu.roll(lengthen(stacked_ref[right, :], size), cut, 0)
            here = slice(pair * size, (pair + 1) * size)
            block(packed_refs, k)[here, :] = jnp.where(packed_index < cut, first, second)

    if not split_up:
        each(sources, unpack)
    picked = jnp.where(lax.broadcasted_iota(jnp.int32, (cells, wells), 0) == wells_ref[...], 1.0, 0.0).astype(BF16)
    turned = (((0,), (0,)), ((), ()))

    def first(k):
        here = pl.ds(k * chunk, chunk)
        high, low = split(u_ref[:, here])
        if split_up:
            part = half_product(rank_pad, 0, u_ref, received_refs[: count // 2], stacked_ref) + far_part_ref[...]
        else:
            part = product_of(high, low, stacked_ref[here, :])
        own = lax.dot_general(picked, high, turned, preferred_element_type=F32).astype(BF16)
        rows_ref[0:wells, here] = own
        rows_ref[wells : 2 * wells, here] = own
        rows_ref[2 * wells :, here] = lax.dot_general(picked, low, turned, preferred_element_type=F32).astype(BF16)
        if depth == chunk:
            field_ref[...] = part
        else:

            @pl.when(k == 0)
            def _():
                field_ref[...] = part

            @pl.when(k > 0)
            def _():
                field_ref[...] += part

    repeat(depth // chunk, first)
    high, rest = split_rest(field_ref[...])
    middle, rest = split_rest(rest)
    parts = jnp.concatenate([high, middle, rest.astype(BF16)], axis=1)
    parts = lax.dot_general(picked, parts, turned, preferred_element_type=F32)
    expo = jnp.exp(parts[:, :width] + parts[:, width : 2 * width] + parts[:, 2 * width :])
    weighted = (expo - observed_ref[...]) * expo / 0.25
    high, low = split(weighted)
    below = jnp.concatenate([high, low, high], axis=0)

    def back(k):
        here = pl.ds(k * chunk, chunk)
        stacked_ref[here, :] = lax.dot_general(rows_ref[:, here], below, turned, preferred_element_type=F32)

    repeat(depth // chunk, back)
    each(sources, pack)


def gradient_part(plan_ref, v_ref, returned_refs, first, ordered_ref, chosen_ref):
    _, local, rank_pad, cells = v_ref.shape
    width = ordered_ref.shape[2]
    packed = packed_rows(rank_pad)
    rank_index = lax.broadcasted_iota(jnp.int32, (rank_pad, width), 0)
    for i, returned_ref in enumerate(returned_refs):
        q = scalar(plan_ref, first + i, 0)
        here = slice(i * rank_pad, (i + 1) * rank_pad)
        for pair in range(local // 2):
            left, right = 2 * pair, 2 * pair + 1
            cut = scalar(plan_ref, first + i, 1 + left)
            both = returned_ref[pair * packed : (pair + 1) * packed, :]
            ordered_ref[left, here, :] = jnp.where(rank_index < cut, both[:rank_pad], 0.0)
            second = pltpu.roll(both, packed - cut, 0)[:rank_pad]
            ordered_ref[right, here, :] = jnp.where(rank_index < scalar(plan_ref, first + i, 1 + right), second, 0.0)
        for j in range(local):
            chosen_ref[j, here, :] = v_ref[q, j]
    return [product(chosen_ref[j], ordered_ref[j], (0, 0)) for j in range(local)]


def gradient_far_kernel(plan_ref, v_ref, *refs):
    returned_refs, (part_ref, ordered_ref, chosen_ref) = refs[:-3], refs[-3:]
    cells = v_ref.shape[3]
    for j, part in enumerate(gradient_part(plan_ref, v_ref, returned_refs, len(returned_refs), ordered_ref, chosen_ref)):
        part_ref[j * cells : (j + 1) * cells, :] = part


def gradient_near_kernel(axis, turn, half, plan_ref, v_ref, latent_ref, part_ref, *refs):
    returned_refs, out_refs, (ordered_ref, chosen_ref, total_ref) = refs[:half], refs[half:-3], refs[-3:]
    cells = v_ref.shape[3]
    for j, part in enumerate(gradient_part(plan_ref, v_ref, returned_refs, 0, ordered_ref, chosen_ref)):
        here = slice(j * cells, (j + 1) * cells)
        total_ref[here, :] = part + part_ref[here, :]
    hand_out(axis, turn, total_ref, latent_ref, out_refs)


def hand_out(axis, turn, total_ref, latent_ref, out_refs):
    me = lax.axis_index(axis)
    size = out_refs[0].shape[0]
    for step, out_ref in enumerate(out_refs):
        there = pl.ds(pl.multiple_of(turn(me, step) * size, size), size)
        if step == 0:
            out_ref[...] = total_ref[there, :] + latent_ref[there, :]
        else:
            out_ref[...] = total_ref[there, :]


def gradient_kernel(group, axis, turn, count, plan_ref, v_ref, latent_ref, *refs):
    returned_refs, out_refs, (ordered_ref, total_ref) = refs[:count], refs[count:-2], refs[-2:]
    rows, local, rank_pad, cells = v_ref.shape
    width = latent_ref.shape[1]
    rank_index = lax.broadcasted_iota(jnp.int32, (rank_pad, width), 0)

    packed = packed_rows(rank_pad)

    def place(k):
        q = scalar(plan_ref, k, 0)
        for pair in range(local // 2):
            left, right = 2 * pair, 2 * pair + 1
            cut = scalar(plan_ref, k, 1 + left)
            both = block(returned_refs, k)[pair * packed : (pair + 1) * packed, :]
            ordered_ref[left, q] = jnp.where(rank_index < cut, both[:rank_pad], 0.0)
            second = pltpu.roll(both, packed - cut, 0)[:rank_pad]
            ordered_ref[right, q] = jnp.where(rank_index < scalar(plan_ref, k, 1 + right), second, 0.0)

    each(rows, place)

    def some(g):
        for j in range(local):
            v_rows = v_ref[pl.ds(g * group, group), j].reshape(group * rank_pad, cells)
            part = product(v_rows, ordered_ref[j, pl.ds(g * group, group)].reshape(group * rank_pad, width), (0, 0))
            here = slice(j * cells, (j + 1) * cells)
            if rows == group:
                total_ref[here, :] = part
            else:

                @pl.when(g == 0)
                def _():
                    total_ref[here, :] = part

                @pl.when(g > 0)
                def _():
                    total_ref[here, :] += part

    repeat(rows // group, some)
    hand_out(axis, turn, total_ref, latent_ref, out_refs)


def exchange(arrays):
    if len(arrays) == 1:
        return [lax.all_to_all(arrays[0], "col", split_axis=0, concat_axis=0, tiled=True)]
    count = len(arrays)
    return [arrays[0]] + [lax.ppermute(arrays[k], "col", [(i, i ^ k) for i in range(count)]) for k in range(1, count)]


def on_device(n_row, latent, v_basis, u_basis, ranks, slot_row, wells, observed):
    rows, _, local, rank_pad, cells = v_basis.shape
    width = latent.shape[1]
    v_rows = v_basis[:, 0]
    u_owned = u_basis[0, 0]
    observed_here = observed[0, 0]
    well_count = observed_here.shape[0]
    pairs, packed = local // 2, packed_rows(rank_pad)
    depth = u_owned.shape[1]
    group = 8 if rows % 8 == 0 else 1
    chunk = 768 if depth % 768 == 0 else depth
    direct = rows <= 8 and rows & (rows - 1) == 0 and rows > 1
    count = rows if direct else 1
    far = [0] + sorted(range(1, count), key=lambda k: (-k.bit_length(), (k & 1) ^ (k.bit_length() == 2), k))

    def carried(size):
        shape = (size, width) if direct else (rows, size, width)
        return [jax.ShapeDtypeStruct(shape, F32)] * count

    def put_back(kernel, before, handed):
        def run(*refs):
            refs = list(refs)
            moved = refs[before : before + len(handed)]
            refs[before : before + len(handed)] = [moved[handed.index(k)] for k in range(len(handed))]
            kernel(*refs)

        return run

    outs = pl.pallas_call(
        functools.partial(blocks_kernel, group),
        out_shape=(
            *carried(pairs * (packed + MARK)),
            jax.ShapeDtypeStruct((rows, 128), jnp.int32),
            jax.ShapeDtypeStruct((1, well_count), jnp.int32),
        ),
        in_specs=[HBM] * 5,
        out_specs=(VMEM,) * (count + 2),
        scratch_shapes=[
            pltpu.VMEM((local, rows, rank_pad, width), F32),
            pltpu.SMEM(slot_row.shape, jnp.int32),
            pltpu.SMEM((local, rows), jnp.int32),
            pltpu.VMEM(latent.shape, F32),
            pltpu.VMEM((local, rows, rank_pad, cells), F32),
            pltpu.SemaphoreType.DMA((2 * local + 3,)),
        ],
        compiler_params=params([latent, v_rows]),
        name="blocks",
    )(stay(slot_row), stay(ranks[:, 0].T), stay(wells[0]), stay(latent), stay(v_rows))
    sent, (plan, wells_here) = outs[:count], outs[count:]
    received = exchange(sent)
    half = count // 2
    first_half = [k for k in far if k < half]
    other_half = [k for k in far if k >= half]
    extra = []
    if direct:
        far_part = pl.pallas_call(
            put_back(functools.partial(owner_far_kernel, rank_pad), 1, [k - half for k in other_half]),
            out_shape=jax.ShapeDtypeStruct((cells, width), F32),
            in_specs=[VMEM] * (1 + half),
            out_specs=VMEM,
            scratch_shapes=[pltpu.VMEM((depth // 2, width), F32)],
            compiler_params=params([u_owned, u_owned]),
            cost_estimate=pl.CostEstimate(flops=3 * cells * depth * width, bytes_accessed=4 * cells * depth, transcendentals=0),
            name="owner_far",
        )(u_owned, *[received[k] for k in other_half])
        extra = [far_part]
    handed = other_half + first_half if direct else far
    field, *adjoint = pl.pallas_call(
        put_back(functools.partial(owner_kernel, chunk, rank_pad, count), 3 + len(extra), handed),
        out_shape=(pltpu.VMEM((cells, width), F32), *carried(pairs * packed)),
        in_specs=[VMEM] * (3 + len(extra) + count),
        out_specs=(VMEM,) * (1 + count),
        scratch_shapes=[pltpu.VMEM((depth, width), F32), pltpu.VMEM((3 * well_count, depth), BF16)],
        compiler_params=params([u_owned, u_owned, observed_here]),
        name="owner",
    )(wells_here, u_owned, observed_here, *extra, *[received[k] for k in handed])
    returned = exchange(adjoint)
    paired = n_row & (n_row - 1) == 0

    def turn(index, step):
        return index ^ step if paired else lax.rem(index + step, n_row)

    size = local * cells // n_row
    part_shape = [jax.ShapeDtypeStruct((size, width), F32)] * n_row
    if direct:
        halves = [pltpu.VMEM((local, half * rank_pad, width), F32), pltpu.VMEM((local, half * rank_pad, cells), F32)]
        far_part = pl.pallas_call(
            put_back(gradient_far_kernel, 2, [k - half for k in other_half]),
            out_shape=jax.ShapeDtypeStruct((local * cells, width), F32),
            in_specs=[VMEM] * (2 + half),
            out_specs=VMEM,
            scratch_shapes=halves,
            compiler_params=params([u_owned, v_rows, latent]),
            cost_estimate=pl.CostEstimate(flops=3 * cells * depth * width, bytes_accessed=4 * cells * depth, transcendentals=0),
            name="gradient_far",
        )(plan, v_rows, *[returned[k] for k in other_half])
        parts = pl.pallas_call(
            put_back(functools.partial(gradient_near_kernel, "row", turn, half), 4, first_half),
            out_shape=part_shape,
            in_specs=[VMEM] * (4 + half),
            out_specs=[VMEM] * n_row,
            scratch_shapes=[*halves, pltpu.VMEM((local * cells, width), F32)],
            compiler_params=params([u_owned, v_rows, latent]),
            name="gradient",
        )(plan, v_rows, latent, far_part, *[returned[k] for k in first_half])
    else:
        parts = pl.pallas_call(
            functools.partial(gradient_kernel, group, "row", turn, count),
            out_shape=part_shape,
            in_specs=[VMEM] * (3 + count),
            out_specs=[VMEM] * n_row,
            scratch_shapes=[pltpu.VMEM((local, rows, rank_pad, width), F32), pltpu.VMEM((local * cells, width), F32)],
            compiler_params=params([u_owned, v_rows, latent]),
            name="gradient",
        )(plan, v_rows, latent, *returned)
    gradient = parts[0]
    for step in range(1, n_row):
        pairs_of = [(i, i ^ step if paired else (i + step) % n_row) for i in range(n_row)]
        gradient = gradient + lax.ppermute(parts[step], "row", pairs_of)
    return field[None, None], gradient


def solution(mesh):
    placed = (
        P("col", None),
        P(None, "row", "col", None, None),
        P("col", "row", None, None),
        P(None, "row", "col"),
        P("row", None),
        P("col", "row", None),
        P("col", "row", None, None),
    )
    return jax.shard_map(
        functools.partial(on_device, mesh.shape["row"]),
        mesh=mesh,
        in_specs=placed,
        out_specs=(P("col", "row", None, None), P(("col", "row"), None)),
        check_vma=False,
    )
```

```python
import functools

import jax
import jax.numpy as jnp
from jax import lax
from jax.experimental import pallas as pl
from jax.experimental.pallas import tpu as pltpu
from jax.sharding import PartitionSpec as P

F32 = jnp.float32
BF16 = jnp.bfloat16
VMEM = pl.BlockSpec(memory_space=pltpu.VMEM)
HBM = pl.BlockSpec(memory_space=pltpu.HBM)
MARK = 8


def split_rest(x):
    high = x.astype(BF16)
    return high, x - high.astype(F32)


def split(x):
    high, rest = split_rest(x)
    return high, rest.astype(BF16)


def product(a, b, contract=(1, 0)):
    return product_of(*split(a), b, contract)


def product_of(a_high, a_low, b, contract=(1, 0)):
    dims = (((contract[0],), (contract[1],)), ((), ()))
    b_high, b_low = split(b)
    both = lax.dot_general(a_high, jnp.concatenate([b_high, b_low], axis=1), dims, preferred_element_type=F32)
    width = b.shape[1]
    return both[:, :width] + both[:, width:] + lax.dot_general(a_low, b_high, dims, preferred_element_type=F32)


def repeat(count, body):
    if count == 1:
        body(0)
    else:
        pl.loop(0, count)(body)


def each(count, body):
    if count <= 16:
        for i in range(count):
            body(i)
    else:
        pl.loop(0, count)(body)


def params(arrays):
    held = sum(a.size * a.dtype.itemsize for a in arrays)
    return pltpu.CompilerParams(vmem_limit_bytes=min(4 * held + (4 << 20), 56 << 20))


def packed_rows(rank_pad):
    return rank_pad + rank_pad // 2


def lengthen(x, size):
    return jnp.concatenate([x, jnp.zeros((size - x.shape[0], x.shape[1]), x.dtype)], axis=0)


def scalar(ref, row, column):
    return ref[pl.ds(row, 1), column : column + 1][0, 0]


def block(refs, k):
    return refs[k] if len(refs) > 1 else refs[0].at[k]


def partner(refs, k):
    return lax.axis_index("col") ^ k if len(refs) > 1 else k


def stay(x):
    return pltpu.with_memory_space_constraint(x, pltpu.HBM)


def blocks_kernel(group, order_hbm, ranks_hbm, wells_hbm, latent_hbm, v_hbm, *refs):
    out_refs, (plan_ref, wells_out, held_ref, order_ref, ranks_ref, latent_ref, v_ref, sems) = refs[:-8], refs[-8:]
    local, rows, rank_pad, cells = v_ref.shape
    width = latent_ref.shape[1]
    small = [
        pltpu.make_async_copy(order_hbm, order_ref, sems.at[2 * local]),
        pltpu.make_async_copy(ranks_hbm, ranks_ref, sems.at[2 * local + 1]),
    ]
    later = [pltpu.make_async_copy(wells_hbm, wells_out, sems.at[2 * local + 2])]
    tiles = []
    for j in range(local):
        here = pl.ds(j * cells, cells)
        tiles.append(
            (
                pltpu.make_async_copy(v_hbm.at[:, j], v_ref.at[j], sems.at[2 * j]),
                pltpu.make_async_copy(latent_hbm.at[here], latent_ref.at[here], sems.at[2 * j + 1]),
            )
        )
    for copies in tiles:
        for copy in copies:
            copy.start()
    for copy in small + later:
        copy.start()
    for j in range(local):
        for copy in tiles[j]:
            copy.wait()

        def some(g):
            v_rows = v_ref[j, pl.ds(g * group, group)].reshape(group * rank_pad, cells)
            made = product(v_rows, latent_ref[j * cells : (j + 1) * cells, :])
            held_ref[j, pl.ds(g * group, group)] = made.reshape(group, rank_pad, width)

        repeat(rows // group, some)
    for copy in small:
        copy.wait()
    rank_index = lax.broadcasted_iota(jnp.int32, (rank_pad, width), 0)
    size = packed_rows(rank_pad)

    lane = lax.broadcasted_iota(jnp.int32, (1, plan_ref.shape[1]), 1)

    def place(k):
        q = order_ref[0, partner(out_refs, k)]
        plan = jnp.where(lane == 0, q, 0)
        for j in range(local):
            plan = jnp.where(lane == 1 + j, ranks_ref[j, q], plan)
        plan_ref[pl.ds(k, 1), :] = plan
        out_ref = block(out_refs, k)
        for pair in range(local // 2):
            left, right = 2 * pair, 2 * pair + 1
            cut = ranks_ref[left, q]
            first = jnp.where(rank_index < cut, held_ref[left, q], 0.0)
            second = jnp.where(rank_index < ranks_ref[right, q], held_ref[right, q], 0.0)
            base = pair * (size + MARK)
            out_ref[base : base + size, :] = lengthen(first, size) + pltpu.roll(lengthen(second, size), cut, 0)
            out_ref[base + size : base + size + MARK, :] = jnp.full((MARK, width), cut.astype(F32))

    each(rows, place)
    for copy in later:
        copy.wait()


def unpack_into(stacked_ref, received_ref, rank_pad, at, pair):
    size = packed_rows(rank_pad)
    width = stacked_ref.shape[1]
    rank_index = lax.broadcasted_iota(jnp.int32, (rank_pad, width), 0)
    base = pair * (size + MARK)
    cut = scalar(received_ref, base + size, 0).astype(jnp.int32)
    both = received_ref[base : base + size, :]
    left = pl.multiple_of(at, 8)
    stacked_ref[pl.ds(left, rank_pad), :] = jnp.where(rank_index < cut, both[:rank_pad], 0.0)
    second = pltpu.roll(both, size - cut, 0)[:rank_pad]
    right = pl.multiple_of(left + rank_pad, 8)
    stacked_ref[pl.ds(right, rank_pad), :] = jnp.where(rank_index < size - cut, second, 0.0)


def half_product(rank_pad, flip, u_ref, received_refs, stacked_ref):
    half = len(received_refs)
    depth = u_ref.shape[1] // 2
    each_rows = depth // half
    me = lax.axis_index("col")
    for k, received_ref in enumerate(received_refs):
        for pair in range(each_rows // (2 * rank_pad)):
            at = ((me ^ k) % half) * each_rows + pair * 2 * rank_pad
            unpack_into(stacked_ref, received_ref, rank_pad, at, pair)
    columns = pl.ds(pl.multiple_of(((me // half) ^ flip) * depth, depth), depth)
    return product(u_ref[:, columns], stacked_ref[:depth, :])


def owner_far_kernel(rank_pad, u_ref, *refs):
    received_refs, (part_ref, stacked_ref) = refs[:-2], refs[-2:]
    part_ref[...] = half_product(rank_pad, 1, u_ref, received_refs, stacked_ref)


def owner_kernel(chunk, rank_pad, count, wells_ref, u_ref, observed_ref, *refs):
    split_up = count > 1
    if split_up:
        far_part_ref, refs = refs[0], refs[1:]
    received_refs, field_ref, packed_refs, (stacked_ref, rows_ref) = (
        refs[:count],
        refs[count],
        refs[count + 1 : 2 * count + 1],
        refs[2 * count + 1 :],
    )
    depth, width = stacked_ref.shape
    wells = observed_ref.shape[0]
    cells = u_ref.shape[0]
    size = packed_rows(rank_pad)
    sources = depth // (received_refs[0].shape[-2] // (size + MARK) * 2 * rank_pad)
    pairs = depth // (sources * 2 * rank_pad)
    rank_index = lax.broadcasted_iota(jnp.int32, (rank_pad, width), 0)
    packed_index = lax.broadcasted_iota(jnp.int32, (size, width), 0)

    def first_rank(k, pair):
        return scalar(block(received_refs, k), pair * (size + MARK) + size, 0).astype(jnp.int32)

    def places(k, pair):
        left = pl.multiple_of((partner(received_refs, k) * pairs + pair) * 2 * rank_pad, 8)
        return pl.ds(left, rank_pad), pl.ds(pl.multiple_of(left + rank_pad, 8), rank_pad)

    def unpack(k):
        for pair in range(pairs):
            cut = first_rank(k, pair)
            both = block(received_refs, k)[pair * (size + MARK) : pair * (size + MARK) + size, :]
            left, right = places(k, pair)
            stacked_ref[left, :] = jnp.where(rank_index < cut, both[:rank_pad], 0.0)
            second = pltpu.roll(both, size - cut, 0)[:rank_pad]
            stacked_ref[right, :] = jnp.where(rank_index < size - cut, second, 0.0)

    def pack(k):
        for pair in range(pairs):
            cut = first_rank(k, pair)
            left, right = places(k, pair)
            first = lengthen(stacked_ref[left, :], size)
            second = pltpu.roll(lengthen(stacked_ref[right, :], size), cut, 0)
            here = slice(pair * size, (pair + 1) * size)
            block(packed_refs, k)[here, :] = jnp.where(packed_index < cut, first, second)

    if not split_up:
        each(sources, unpack)
    picked = jnp.where(lax.broadcasted_iota(jnp.int32, (cells, wells), 0) == wells_ref[...], 1.0, 0.0).astype(BF16)
    turned = (((0,), (0,)), ((), ()))

    def first(k):
        here = pl.ds(k * chunk, chunk)
        high, low = split(u_ref[:, here])
        if split_up:
            part = half_product(rank_pad, 0, u_ref, received_refs[: count // 2], stacked_ref) + far_part_ref[...]
        else:
            part = product_of(high, low, stacked_ref[here, :])
        own = lax.dot_general(picked, high, turned, preferred_element_type=F32).astype(BF16)
        rows_ref[0:wells, here] = own
        rows_ref[wells : 2 * wells, here] = own
        rows_ref[2 * wells :, here] = lax.dot_general(picked, low, turned, preferred_element_type=F32).astype(BF16)
        if depth == chunk:
            field_ref[...] = part
        else:

            @pl.when(k == 0)
            def _():
                field_ref[...] = part

            @pl.when(k > 0)
            def _():
                field_ref[...] += part

    repeat(depth // chunk, first)
    high, rest = split_rest(field_ref[...])
    middle, rest = split_rest(rest)
    parts = jnp.concatenate([high, middle, rest.astype(BF16)], axis=1)
    parts = lax.dot_general(picked, parts, turned, preferred_element_type=F32)
    expo = jnp.exp(parts[:, :width] + parts[:, width : 2 * width] + parts[:, 2 * width :])
    weighted = (expo - observed_ref[...]) * expo / 0.25
    high, low = split(weighted)
    below = jnp.concatenate([high, low, high], axis=0)

    def back(k):
        here = pl.ds(k * chunk, chunk)
        stacked_ref[here, :] = lax.dot_general(rows_ref[:, here], below, turned, preferred_element_type=F32)

    repeat(depth // chunk, back)
    each(sources, pack)


def gradient_part(plan_ref, v_ref, returned_refs, first, ordered_ref, chosen_ref):
    _, local, rank_pad, cells = v_ref.shape
    width = ordered_ref.shape[2]
    packed = packed_rows(rank_pad)
    rank_index = lax.broadcasted_iota(jnp.int32, (rank_pad, width), 0)
    for i, returned_ref in enumerate(returned_refs):
        q = scalar(plan_ref, first + i, 0)
        here = slice(i * rank_pad, (i + 1) * rank_pad)
        for pair in range(local // 2):
            left, right = 2 * pair, 2 * pair + 1
            cut = scalar(plan_ref, first + i, 1 + left)
            both = returned_ref[pair * packed : (pair + 1) * packed, :]
            ordered_ref[left, here, :] = jnp.where(rank_index < cut, both[:rank_pad], 0.0)
            second = pltpu.roll(both, packed - cut, 0)[:rank_pad]
            ordered_ref[right, here, :] = jnp.where(rank_index < scalar(plan_ref, first + i, 1 + right), second, 0.0)
        for j in range(local):
            chosen_ref[j, here, :] = v_ref[q, j]
    return [product(chosen_ref[j], ordered_ref[j], (0, 0)) for j in range(local)]


def gradient_far_kernel(plan_ref, v_ref, *refs):
    returned_refs, (part_ref, ordered_ref, chosen_ref) = refs[:-3], refs[-3:]
    cells = v_ref.shape[3]
    for j, part in enumerate(gradient_part(plan_ref, v_ref, returned_refs, len(returned_refs), ordered_ref, chosen_ref)):
        part_ref[j * cells : (j + 1) * cells, :] = part


def gradient_near_kernel(axis, turn, half, plan_ref, v_ref, latent_ref, part_ref, *refs):
    returned_refs, out_refs, (ordered_ref, chosen_ref, total_ref) = refs[:half], refs[half:-3], refs[-3:]
    cells = v_ref.shape[3]
    for j, part in enumerate(gradient_part(plan_ref, v_ref, returned_refs, 0, ordered_ref, chosen_ref)):
        here = slice(j * cells, (j + 1) * cells)
        total_ref[here, :] = part + part_ref[here, :]
    hand_out(axis, turn, total_ref, latent_ref, out_refs)


def hand_out(axis, turn, total_ref, latent_ref, out_refs):
    me = lax.axis_index(axis)
    size = out_refs[0].shape[0]
    for step, out_ref in enumerate(out_refs):
        there = pl.ds(pl.multiple_of(turn(me, step) * size, size), size)
        if step == 0:
            out_ref[...] = total_ref[there, :] + latent_ref[there, :]
        else:
            out_ref[...] = total_ref[there, :]


def gradient_kernel(group, axis, turn, count, plan_ref, v_ref, latent_ref, *refs):
    returned_refs, out_refs, (ordered_ref, total_ref) = refs[:count], refs[count:-2], refs[-2:]
    rows, local, rank_pad, cells = v_ref.shape
    width = latent_ref.shape[1]
    rank_index = lax.broadcasted_iota(jnp.int32, (rank_pad, width), 0)

    packed = packed_rows(rank_pad)

    def place(k):
        q = scalar(plan_ref, k, 0)
        for pair in range(local // 2):
            left, right = 2 * pair, 2 * pair + 1
            cut = scalar(plan_ref, k, 1 + left)
            both = block(returned_refs, k)[pair * packed : (pair + 1) * packed, :]
            ordered_ref[left, q] = jnp.where(rank_index < cut, both[:rank_pad], 0.0)
            second = pltpu.roll(both, packed - cut, 0)[:rank_pad]
            ordered_ref[right, q] = jnp.where(rank_index < scalar(plan_ref, k, 1 + right), second, 0.0)

    each(rows, place)

    def some(g):
        for j in range(local):
            v_rows = v_ref[pl.ds(g * group, group), j].reshape(group * rank_pad, cells)
            part = product(v_rows, ordered_ref[j, pl.ds(g * group, group)].reshape(group * rank_pad, width), (0, 0))
            here = slice(j * cells, (j + 1) * cells)
            if rows == group:
                total_ref[here, :] = part
            else:

                @pl.when(g == 0)
                def _():
                    total_ref[here, :] = part

                @pl.when(g > 0)
                def _():
                    total_ref[here, :] += part

    repeat(rows // group, some)
    hand_out(axis, turn, total_ref, latent_ref, out_refs)


def exchange(arrays):
    if len(arrays) == 1:
        return [lax.all_to_all(arrays[0], "col", split_axis=0, concat_axis=0, tiled=True)]
    count = len(arrays)
    return [arrays[0]] + [lax.ppermute(arrays[k], "col", [(i, i ^ k) for i in range(count)]) for k in range(1, count)]


def on_device(n_row, latent, v_basis, u_basis, ranks, slot_row, wells, observed):
    rows, _, local, rank_pad, cells = v_basis.shape
    width = latent.shape[1]
    v_rows = v_basis[:, 0]
    u_owned = u_basis[0, 0]
    observed_here = observed[0, 0]
    well_count = observed_here.shape[0]
    pairs, packed = local // 2, packed_rows(rank_pad)
    depth = u_owned.shape[1]
    group = 8 if rows % 8 == 0 else 1
    chunk = 768 if depth % 768 == 0 else depth
    direct = rows <= 8 and rows & (rows - 1) == 0 and rows > 1
    count = rows if direct else 1
    far = [0] + sorted(range(1, count), key=lambda k: (-k.bit_length(), (k & 1) ^ (k.bit_length() == 2), k))

    def carried(size):
        shape = (size, width) if direct else (rows, size, width)
        return [jax.ShapeDtypeStruct(shape, F32)] * count

    def put_back(kernel, before, handed):
        def run(*refs):
            refs = list(refs)
            moved = refs[before : before + len(handed)]
            refs[before : before + len(handed)] = [moved[handed.index(k)] for k in range(len(handed))]
            kernel(*refs)

        return run

    outs = pl.pallas_call(
        functools.partial(blocks_kernel, group),
        out_shape=(
            *carried(pairs * (packed + MARK)),
            jax.ShapeDtypeStruct((rows, 128), jnp.int32),
            jax.ShapeDtypeStruct((1, well_count), jnp.int32),
        ),
        in_specs=[HBM] * 5,
        out_specs=(VMEM,) * (count + 2),
        scratch_shapes=[
            pltpu.VMEM((local, rows, rank_pad, width), F32),
            pltpu.SMEM(slot_row.shape, jnp.int32),
            pltpu.SMEM((local, rows), jnp.int32),
            pltpu.VMEM(latent.shape, F32),
            pltpu.VMEM((local, rows, rank_pad, cells), F32),
            pltpu.SemaphoreType.DMA((2 * local + 3,)),
        ],
        compiler_params=params([latent, v_rows]),
        name="blocks",
    )(stay(slot_row), stay(ranks[:, 0].T), stay(wells[0]), stay(latent), stay(v_rows))
    sent, (plan, wells_here) = outs[:count], outs[count:]
    received = exchange(sent)
    half = count // 2
    first_half = [k for k in far if k < half]
    other_half = [k for k in far if k >= half]
    extra = []
    if direct:
        far_part = pl.pallas_call(
            put_back(functools.partial(owner_far_kernel, rank_pad), 1, [k - half for k in other_half]),
            out_shape=jax.ShapeDtypeStruct((cells, width), F32),
            in_specs=[VMEM] * (1 + half),
            out_specs=VMEM,
            scratch_shapes=[pltpu.VMEM((depth // 2, width), F32)],
            compiler_params=params([u_owned, u_owned]),
            cost_estimate=pl.CostEstimate(flops=3 * cells * depth * width, bytes_accessed=4 * cells * depth, transcendentals=0),
            name="owner_far",
        )(u_owned, *[received[k] for k in other_half])
        extra = [far_part]
    handed = other_half + first_half if direct else far
    field, *adjoint = pl.pallas_call(
        put_back(functools.partial(owner_kernel, chunk, rank_pad, count), 3 + len(extra), handed),
        out_shape=(pltpu.VMEM((cells, width), F32), *carried(pairs * packed)),
        in_specs=[VMEM] * (3 + len(extra) + count),
        out_specs=(VMEM,) * (1 + count),
        scratch_shapes=[pltpu.VMEM((depth, width), F32), pltpu.VMEM((3 * well_count, depth), BF16)],
        compiler_params=params([u_owned, u_owned, observed_here]),
        name="owner",
    )(wells_here, u_owned, observed_here, *extra, *[received[k] for k in handed])
    returned = exchange(adjoint)
    paired = n_row & (n_row - 1) == 0

    def turn(index, step):
        return index ^ step if paired else lax.rem(index + step, n_row)

    size = local * cells // n_row
    part_shape = [jax.ShapeDtypeStruct((size, width), F32)] * n_row
    if direct:
        halves = [pltpu.VMEM((local, half * rank_pad, width), F32), pltpu.VMEM((local, half * rank_pad, cells), F32)]
        far_part = pl.pallas_call(
            put_back(gradient_far_kernel, 2, [k - half for k in other_half]),
            out_shape=jax.ShapeDtypeStruct((local * cells, width), F32),
            in_specs=[VMEM] * (2 + half),
            out_specs=VMEM,
            scratch_shapes=halves,
            compiler_params=params([u_owned, v_rows, latent]),
            cost_estimate=pl.CostEstimate(flops=3 * cells * depth * width, bytes_accessed=4 * cells * depth, transcendentals=0),
            name="gradient_far",
        )(plan, v_rows, *[returned[k] for k in other_half])
        parts = pl.pallas_call(
            put_back(functools.partial(gradient_near_kernel, "row", turn, half), 4, first_half),
            out_shape=part_shape,
            in_specs=[VMEM] * (4 + half),
            out_specs=[VMEM] * n_row,
            scratch_shapes=[*halves, pltpu.VMEM((local * cells, width), F32)],
            compiler_params=params([u_owned, v_rows, latent]),
            name="gradient",
        )(plan, v_rows, latent, far_part, *[returned[k] for k in first_half])
    else:
        parts = pl.pallas_call(
            functools.partial(gradient_kernel, group, "row", turn, count),
            out_shape=part_shape,
            in_specs=[VMEM] * (3 + count),
            out_specs=[VMEM] * n_row,
            scratch_shapes=[pltpu.VMEM((local, rows, rank_pad, width), F32), pltpu.VMEM((local * cells, width), F32)],
            compiler_params=params([u_owned, v_rows, latent]),
            name="gradient",
        )(plan, v_rows, latent, *returned)
    parts = list(parts)
    if paired:
        bit = 1
        while bit < n_row:
            pairs_of = [(i, i ^ bit) for i in range(n_row)]
            kept = [k for k in range(0, n_row, bit) if not k & bit]
            for k in reversed(kept):
                parts[k] = parts[k] + lax.ppermute(parts[k | bit], "row", pairs_of)
            bit *= 2
        gradient = parts[0]
    else:
        gradient = parts[0]
        for step in range(1, n_row):
            gradient = gradient + lax.ppermute(parts[step], "row", [(i, (i + step) % n_row) for i in range(n_row)])
    return field[None, None], gradient


def solution(mesh):
    placed = (
        P("col", None),
        P(None, "row", "col", None, None),
        P("col", "row", None, None),
        P(None, "row", "col"),
        P("row", None),
        P("col", "row", None),
        P("col", "row", None, None),
    )
    return jax.shard_map(
        functools.partial(on_device, mesh.shape["row"]),
        mesh=mesh,
        in_specs=placed,
        out_specs=(P("col", "row", None, None), P(("col", "row"), None)),
        check_vma=False,
    )
```
